128 devices in a mesh: band: 4 (over x_lo, core), slab: 32 (over x_hi, z, y).
Axes of the slice: x: 4 (x_hi: 2, x_lo: 2; x = x_hi * 2 + x_lo), y: 4, z: 4, core: 2. Of those that a mesh axis runs over, the one named last changes fastest.
Arguments:
- resident: float32 [8, 128, 128, 128], P('band', 'slab'), may hold values from -5 to 5
- blocks: float32 [16, 128, 128, 128], P('band', 'slab'), may hold values from -5 to 5
- occupation: float32 [16], replicated, may hold values from 0.25 to 1
Outputs:
- exchange_term: float32 [8, 128, 128, 128], P('band', 'slab')
The draws below stay inside these ranges and needn't reach their ends.
All inputs are finite; a program needn't handle non-finite values.
Results may differ from the reference program's by a relative error of at most 0.0001.
Values sent between devices are 32-bit elements; how exact they have to be, the bound alone decides.
A program may use at most 128 MiB of HBM per device.

```python
import math
import jax
import jax.numpy as jnp
from jax import lax

GRID = 128
SRC = 16
ORBS = 8


def shard_levels(key, dims, split, smallest, high):
    gain, own = 1.0, jax.random.fold_in(key, 6)
    for dim, shards_of in split:
        steps = jnp.exp(jax.random.uniform(jax.random.fold_in(own, dim), (shards_of,), jnp.float32, smallest / len(split), high / len(split)))
        gain = gain * jnp.repeat(steps, dims[dim] // shards_of).reshape([-1 if axis == dim else 1 for axis in range(len(dims))])
    return gain


def bell_draw(rng, dims, spread, limit, pieces=(), held_as=jnp.bfloat16):
    result = spread * jax.random.normal(rng, dims, jnp.float32)
    if pieces:
        result = result * shard_levels(rng, dims, pieces, -0.22, 0.18)
    return jnp.clip(result, -limit, limit).astype(held_as)


def setup_inputs(seed: int = 0) -> dict:
    key_of = jax.random.split(jax.random.key(seed), 4)
    return {
        "resident": bell_draw(key_of[0], (ORBS, GRID, GRID, GRID), 0.35, 5.0, ((0, 4), (1, 32)), jnp.float32),
        "blocks": bell_draw(key_of[1], (SRC, GRID, GRID, GRID), 0.35, 5.0, ((0, 4), (1, 32)), jnp.float32),
        "occupation": jnp.clip(jnp.exp(jax.random.uniform(key_of[2], (SRC,), jnp.float32, math.log(0.25), math.log(1.0))), 0.25, 1.0),
    }


KAPPA_SQ = 0.01


def wave_numbers(grid_len):
    freqs = jnp.fft.fftfreq(grid_len) * (2.0 * math.pi)
    return freqs.astype(jnp.float32)


def coulomb_kernel():
    waves = wave_numbers(GRID)
    squared = waves[:, None, None] ** 2 + waves[None, :, None] ** 2 + waves[None, None, :] ** 2
    return (4.0 * math.pi) / (squared + KAPPA_SQ)


def reference(resident, blocks, occupation):
    source = blocks
    kernel = coulomb_kernel()

    def one_orbital(orbital):
        def accumulate(running, inputs):
            block_orb, weight = inputs
            density = orbital * block_orb
            potential = jnp.fft.ifftn(kernel * jnp.fft.fftn(density)).real.astype(jnp.float32)
            return running - weight * potential * block_orb, None

        running, _ = lax.scan(accumulate, jnp.zeros_like(orbital), (source, occupation))
        return running

    return lax.map(one_orbital, resident)
```

```python
import functools
import math

import jax
import numpy as np
import jax.numpy as jnp
from jax import lax
from jax.experimental import pallas as pl
from jax.experimental.pallas import tpu as pltpu
from jax.sharding import PartitionSpec as P

MESH = pl.DeviceIdType.MESH
PLANES = 4
HALF = PLANES // 2


class Place:
    def __init__(self):
        self.band = lax.axis_index("band")
        slab = lax.axis_index("slab")
        self.core = self.band % 2
        self.half = slab // 16
        self.z = (slab // 4) % 4
        self.y = slab % 4
        self.x = self.half * 2 + self.band // 2

    def device(self, dx=0, dy=0, dz=0, flip=False):
        x, y, z = (self.x + dx) % 4, (self.y + dy) % 4, (self.z + dz) % 4
        core = 1 - self.core if flip else self.core
        return ((x % 2) * 2 + core, (x // 2) * 16 + z * 4 + y)

    def piece(self, half, dy=0, dz=0):
        return half * 16 + ((self.z + dz) % 4) * 4 + (self.y + dy) % 4


class Mail:
    def __init__(self, send_sem, recv_sem):
        self.send_sem, self.recv_sem = send_sem, recv_sem
        self.count = 0
        self.sent = []

    def send(self, src, dst, device):
        number = self.count
        self.count += 1
        copy = pltpu.make_async_remote_copy(
            src_ref=src,
            dst_ref=dst,
            send_sem=self.send_sem.at[number],
            recv_sem=self.recv_sem.at[number],
            device_id=device,
            device_id_type=MESH,
        )
        copy.start()
        self.sent.append(copy)
        return number

    def arrive(self, number, dst, device):
        pltpu.make_async_remote_copy(
            src_ref=dst,
            dst_ref=dst,
            send_sem=self.send_sem.at[number],
            recv_sem=self.recv_sem.at[number],
            device_id=device,
            device_id_type=MESH,
        ).wait_recv()

    def finish(self):
        for copy in self.sent:
            copy.wait_send()


def planes(ref, piece, part=None):
    if part is None:
        return ref.at[pl.ds(piece * PLANES, PLANES)]
    return ref.at[pl.ds(piece * PLANES + part * HALF, HALF)]


def greet(me):
    barrier = pltpu.get_barrier_semaphore()
    near = [me.device(dx=1), me.device(dx=3), me.device(dy=1), me.device(dy=3),
            me.device(dz=1), me.device(dz=3), me.device(dx=2), me.device(flip=True)]
    for other in near:
        pl.semaphore_signal(barrier, inc=1, device_id=other, device_id_type=MESH)
    for k in range(1, 4):
        pl.semaphore_signal(barrier, inc=1, device_id=align_device(me, k), device_id_type=MESH)

    @pl.when(me.band != me.z)
    def _():
        pl.semaphore_signal(barrier, inc=1, device_id=align_device(me, 0), device_id_type=MESH)
        pl.semaphore_wait(barrier, len(near) + 4)

    @pl.when(me.band == me.z)
    def _():
        pl.semaphore_wait(barrier, len(near) + 3)


def align_device(me, step):
    return (me.z, me.half * 16 + me.band * 4 + (me.y + step) % 4)


class Tree:
    def __init__(self, me, mail, full, half, first):
        self.me, self.mail, self.full, self.half = me, mail, full, half
        self.first = first
        self.box = {}

    def off(self, f, s):
        return dict(dy=f % 4, dz=s % 4) if self.first == "y" else dict(dy=s % 4, dz=f % 4)

    def ref(self, f, s, part=None):
        return planes(self.full, self.me.piece(self.half, **self.off(f, s)), part)

    def push(self, key, src, f, s, df, ds, part=None):
        dst = self.ref(f, s, part)
        self.box[key] = self.mail.send(dst if src is None else src, dst, self.me.device(**self.off(df, ds)))

    def take(self, key, f, s, part=None):
        self.mail.arrive(self.box[key], self.ref(f, s, part), self.me.device(**self.off(0, 0)))

    def start(self, src):
        for d in (1, -1):
            self.push(("f", d), src, 0, 0, d, 0)
        for d in (1, -1):
            self.push(("s", 0, d), src, 0, 0, 0, d)

    def row(self):
        for d in (1, -1):
            self.take(("f", d), -d, 0)
            part = 0 if d == 1 else 1
            self.push(("f2", d), None, -d, 0, d, 0, part)
            for e in (1, -1):
                self.push(("s", -d, e), None, -d, 0, 0, e)

    def column(self, f):
        for e in (1, -1):
            self.take(("s", f, e), f, -e)
            part = 0 if e == 1 else 1
            self.push(("s2", f, e), None, f, -e, 0, e, part)

    def far(self):
        for d in (1, -1):
            self.take(("f2", d), 2, 0, 0 if d == 1 else 1)
        for e in (1, -1):
            self.push(("s", 2, e), None, 2, 0, 0, e)

    def last(self, f):
        for e in (1, -1):
            self.take(("s2", f, e), f, 2, 0 if e == 1 else 1)


def gather_kernel(res_ref, blk_ref, rfull, sfull, send_sem, recv_sem, local_sem):
    me = Place()
    greet(me)
    mail = Mail(send_sem, recv_sem)
    h = me.half
    mine = me.piece(h)

    def spiece(dx, flip, t):
        x = (me.x + dx) % 4
        core = 1 - me.core if flip else me.core
        return (x // 2) * 16 + ((x % 2) * 2 + core) * 4 + (me.y + t) % 4

    order = (0, 1, 3, 2)
    align_no = {}
    for t in order:
        number = mail.count
        mail.count += 1
        align_no[t] = number
        src = blk_ref.at[(me.y + t) % 4]
        dst = planes(sfull, mine)

        def remote(src=src, dst=dst, t=t, number=number):
            return pltpu.make_async_remote_copy(
                src_ref=src, dst_ref=dst, send_sem=send_sem.at[number], recv_sem=recv_sem.at[number],
                device_id=align_device(me, t), device_id_type=MESH)
        if t:
            copy = remote()
            copy.start()
            mail.sent.append(copy)
        else:
            @pl.when(me.band != me.z)
            def _():
                remote().start()

            @pl.when(me.band == me.z)
            def _():
                pltpu.make_async_copy(src, dst, local_sem.at[1]).start()
            zero = (remote, src, dst)
    swap = mail.send(res_ref.at[1 - h], planes(rfull, mine), me.device(dx=2))
    tree_a = Tree(me, mail, rfull, h, "y")
    tree_b = Tree(me, mail, rfull, 1 - h, "z")
    tree_a.start(res_ref.at[h])
    own = pltpu.make_async_copy(res_ref.at[h], planes(rfull, mine), local_sem.at[0])
    own.start()
    mail.arrive(swap, planes(rfull, me.piece(1 - h)), me.device(dx=2))
    tree_b.start(None)

    xs = {}
    for t in order:
        back = -t % 4
        dst = planes(sfull, spiece(0, False, back))
        if t:
            mail.arrive(align_no[t], dst, align_device(me, back))
        else:
            @pl.when(me.band != me.z)
            def _():
                zero[0]().wait_recv()

            @pl.when(me.band == me.z)
            def _():
                pltpu.make_async_copy(zero[1], zero[2], local_sem.at[1]).wait()
        for d in (1, -1):
            xs[("x", d, back)] = mail.send(dst, dst, me.device(dx=d))
        xs[("c", 0, back)] = mail.send(dst, dst, me.device(flip=True))
    backs = [-t % 4 for t in order]
    tree_a.row()
    tree_b.row()
    tree_a.column(0)
    tree_b.column(0)
    for t in backs:
        for d in (1, -1):
            ref = planes(sfull, spiece(-d, False, t))
            mail.arrive(xs[("x", d, t)], ref, me.device(dx=-d))
            part = 0 if d == 1 else 1
            ref2 = planes(sfull, spiece(-d, False, t), part)
            xs[("x2", d, t)] = mail.send(ref2, ref2, me.device(dx=d))
            xs[("c", -d, t)] = mail.send(ref, ref, me.device(flip=True))
    tree_a.far()
    tree_b.far()
    for d in (-1, 1):
        tree_a.column(d)
        tree_b.column(d)
    for t in backs:
        for d in (1, -1):
            ref2 = planes(sfull, spiece(2, False, t), 0 if d == 1 else 1)
            mail.arrive(xs[("x2", d, t)], ref2, me.device(dx=-d))
        ref = planes(sfull, spiece(2, False, t))
        xs[("c", 2, t)] = mail.send(ref, ref, me.device(flip=True))
    tree_a.column(2)
    tree_b.column(2)
    for f in (0, -1, 1, 2):
        tree_a.last(f)
        tree_b.last(f)
    for dx in (0, -1, 1, 2):
        for t in backs:
            mail.arrive(xs[("c", dx, t)], planes(sfull, spiece(dx, True, t)), me.device(flip=True))
    own.wait()
    mail.finish()

    @pl.when(me.band != me.z)
    def _():
        zero[0]().wait_send()


MESSAGES = 77


def gather(resident, blocks):
    n = resident.shape[2]
    full = jax.ShapeDtypeStruct((128, n, resident.shape[3]), jnp.float32)
    return pl.pallas_call(
        gather_kernel,
        out_shape=(full, full),
        in_specs=[pl.BlockSpec(memory_space=pl.ANY)] * 2,
        out_specs=(pl.BlockSpec(memory_space=pl.ANY),) * 2,
        scratch_shapes=[
            pltpu.SemaphoreType.DMA((MESSAGES,)),
            pltpu.SemaphoreType.DMA((MESSAGES,)),
            pltpu.SemaphoreType.DMA((2,)),
        ],
        compiler_params=pltpu.CompilerParams(collective_id=0, has_side_effects=True),
        name="gather",
    )(resident, blocks)


class Sum:
    def __init__(self, me, mail, term, near_s, far_s, near_f, far_f, half, first):
        self.me, self.mail, self.term = me, mail, term
        self.near_s, self.far_s, self.near_f, self.far_f = near_s, far_s, near_f, far_f
        self.half, self.first = half, first
        self.box = {}

    def off(self, f, s):
        return dict(dy=f % 4, dz=s % 4) if self.first == "y" else dict(dy=s % 4, dz=f % 4)

    def ref(self, f, s, part=None):
        return planes(self.term, self.me.piece(self.half, **self.off(f, s)), part)

    def slots(self, d, f=None):
        n = 0 if d == 1 else 1
        if f is None:
            return self.far_f.at[n], self.near_f.at[n]
        return self.far_s.at[f % 4, n], self.near_s.at[f % 4, n]

    def post(self, key, src, dst, df, ds):
        self.box[key] = self.mail.send(src, dst, self.me.device(**self.off(df, ds)))

    def add(self, key, into, slot):
        self.mail.arrive(self.box[key], slot, self.me.device())
        into[...] += slot[...]

    def far_column(self, f):
        for e in (1, -1):
            self.post(("a", f, e), self.ref(f, 2, 0 if e == 1 else 1), self.slots(e, f)[0], 0, e)

    def near_column(self, f):
        for e in (1, -1):
            self.add(("a", f, e), self.ref(f, e, 0 if e == 1 else 1), self.slots(e, f)[0])
            self.post(("b", f, e), self.ref(f, e), self.slots(e, f)[1], 0, e)

    def own_column(self, f):
        for e in (1, -1):
            self.add(("b", f, e), self.ref(f, 0), self.slots(e, f)[1])

    def far_row(self):
        for d in (1, -1):
            self.post(("c", d), self.ref(2, 0, 0 if d == 1 else 1), self.slots(d)[0], d, 0)

    def near_row(self, d):
        self.add(("c", d), self.ref(d, 0, 0 if d == 1 else 1), self.slots(d)[0])
        self.post(("d", d), self.ref(d, 0), self.slots(d)[1], d, 0)

    def own_row(self):
        for d in (1, -1):
            self.add(("d", d), self.ref(0, 0), self.slots(d)[1])


def greet_sum(me):
    barrier = pltpu.get_barrier_semaphore()
    near = [me.device(dy=1), me.device(dy=3), me.device(dz=1), me.device(dz=3), me.device(dx=2)]
    for other in near:
        pl.semaphore_signal(barrier, inc=1, device_id=other, device_id_type=MESH)
    pl.semaphore_wait(barrier, len(near))


def sum_kernel(term_ref, out_ref, near_s, far_s, near_f, far_f, send_sem, recv_sem):
    me = Place()
    greet_sum(me)
    mail = Mail(send_sem, recv_sem)
    h = me.half
    sums = [
        Sum(me, mail, term_ref, near_s.at[n], far_s.at[n], near_f.at[n], far_f.at[n], half, first)
        for n, (half, first) in enumerate(((1 - h, "z"), (h, "y")))
    ]
    order = (2, 1, -1, 0)
    for f in order:
        for s in sums:
            s.far_column(f)
    for f in order:
        for s in sums:
            s.near_column(f)
    for f in order:
        for s in sums:
            s.own_column(f)
        for s in sums:
            if f == 2:
                s.far_row()
            elif f:
                s.near_row(f)
    for s in sums:
        s.own_row()
    away = planes(term_ref, me.piece(1 - h))
    swap = mail.send(away, out_ref.at[h], me.device(dx=2))
    out_ref[h] = planes(term_ref, me.piece(h))[...]
    mail.arrive(swap, out_ref.at[1 - h], me.device(dx=2))
    mail.finish()


SUM_MESSAGES = 41


def reduce_term(term):
    n, m = term.shape[1:]
    vmem = pl.BlockSpec(memory_space=pltpu.VMEM)
    return pl.pallas_call(
        sum_kernel,
        out_shape=jax.ShapeDtypeStruct((2, PLANES, n, m), jnp.float32),
        in_specs=[vmem],
        out_specs=vmem,
        scratch_shapes=[
            pltpu.VMEM((2, 4, 2, PLANES, n, m), jnp.float32),
            pltpu.VMEM((2, 4, 2, HALF, n, m), jnp.float32),
            pltpu.VMEM((2, 2, PLANES, n, m), jnp.float32),
            pltpu.VMEM((2, 2, HALF, n, m), jnp.float32),
            pltpu.SemaphoreType.DMA((SUM_MESSAGES,)),
            pltpu.SemaphoreType.DMA((SUM_MESSAGES,)),
        ],
        compiler_params=pltpu.CompilerParams(
            collective_id=1, has_side_effects=True, vmem_limit_bytes=40 * 2**20
        ),
        name="reduce_term",
    )(term)


def basis(n):
    points = np.arange(n)
    freqs = np.arange(n)
    freqs = np.where(freqs > n // 2, n - freqs, freqs)
    angles = 2.0 * np.pi * ((points[:, None] * freqs[None, :]) % n) / n
    table = np.where(np.arange(n)[None, :] > n // 2, np.sin(angles), np.cos(angles)) * np.sqrt(2.0 / n)
    table[:, 0] = 1.0 / np.sqrt(n)
    table[:, n // 2] = np.where(points % 2 == 0, 1.0, -1.0) / np.sqrt(n)
    waves = (freqs * (2.0 * np.pi / n)) ** 2
    return table.astype(np.float32), waves.astype(np.float32)


KAPPA_SQ = 0.01


def apply_pair(orbital, source, weight):
    table, waves = basis(orbital.shape[0])
    table, waves = jnp.asarray(table), jnp.asarray(waves)

    def along(form, values, t):
        return jnp.einsum(form, values, t, precision=lax.Precision.HIGHEST, preferred_element_type=jnp.float32)

    v = orbital * source
    v = along("zyx,xk->zyk", v, table)
    v = along("zyx,yk->zkx", v, table)
    v = along("zyx,zk->kyx", v, table)
    v = v * (4.0 * math.pi / (waves[:, None, None] + waves[None, :, None] + waves[None, None, :] + KAPPA_SQ))
    v = along("zyx,kz->kyx", v, table)
    v = along("zyx,ky->zkx", v, table)
    v = along("zyx,kx->zyk", v, table)
    return v * source * (-weight)


def per_device(resident, blocks, occupation):
    orbital, source = gather(resident, blocks)
    slab = lax.axis_index("slab")
    weight = lax.dynamic_index_in_dim(occupation, slab % 16, 0, False)
    term = apply_pair(orbital, source, weight)
    return reduce_term(term)


def solution(mesh):
    placed = (P("band", "slab", None, None), P("band", "slab", None, None), P())
    return jax.shard_map(
        per_device,
        mesh=mesh,
        in_specs=placed,
        out_specs=P("band", "slab", None, None),
        check_vma=False,
    )
```

```python
import math

import jax
import ml_dtypes
import numpy as np
import jax.numpy as jnp
from jax import lax
from jax.experimental import pallas as pl
from jax.experimental.pallas import tpu as pltpu
from jax.sharding import PartitionSpec as P

MESH = pl.DeviceIdType.MESH
PLANES = 4
GRID = 128
ROWS = PLANES * GRID
HALF = ROWS // 2
KAPPA_SQ = 0.01


class Place:
    def __init__(self):
        self.band = lax.axis_index("band")
        slab = lax.axis_index("slab")
        self.core = self.band % 2
        self.half = slab // 16
        self.z = (slab // 4) % 4
        self.y = slab % 4
        self.x = self.half * 2 + self.band // 2

    def device(self, dx=0, dy=0, dz=0, flip=False):
        x, y, z = (self.x + dx) % 4, (self.y + dy) % 4, (self.z + dz) % 4
        core = 1 - self.core if flip else self.core
        return ((x % 2) * 2 + core, (x // 2) * 16 + z * 4 + y)

    def piece(self, half, dy=0, dz=0):
        return half * 16 + ((self.z + dz) % 4) * 4 + (self.y + dy) % 4


class Mail:
    def __init__(self, send_sem, recv_sem):
        self.send_sem, self.recv_sem = send_sem, recv_sem
        self.count = 0
        self.sent = []

    def send(self, src, dst, device):
        number = self.count
        self.count += 1
        copy = pltpu.make_async_remote_copy(
            src_ref=src,
            dst_ref=dst,
            send_sem=self.send_sem.at[number],
            recv_sem=self.recv_sem.at[number],
            device_id=device,
            device_id_type=MESH,
        )
        copy.start()
        self.sent.append(copy)
        return number

    def arrive(self, number, dst, device):
        pltpu.make_async_remote_copy(
            src_ref=dst,
            dst_ref=dst,
            send_sem=self.send_sem.at[number],
            recv_sem=self.recv_sem.at[number],
            device_id=device,
            device_id_type=MESH,
        ).wait_recv()

    def finish(self):
        for copy in self.sent:
            copy.wait_send()


def planes(ref, piece, part=None):
    if part is None:
        return ref.at[pl.ds(piece * ROWS, ROWS)]
    return ref.at[pl.ds(piece * ROWS + part * HALF, HALF)]


def greet(me):
    barrier = pltpu.get_barrier_semaphore()
    near = [me.device(dx=1), me.device(dx=3), me.device(dy=1), me.device(dy=3),
            me.device(dz=1), me.device(dz=3), me.device(dx=2), me.device(flip=True)]
    for other in near:
        pl.semaphore_signal(barrier, inc=1, device_id=other, device_id_type=MESH)
    for k in range(1, 4):
        pl.semaphore_signal(barrier, inc=1, device_id=align_device(me, k), device_id_type=MESH)

    @pl.when(me.band != me.z)
    def _():
        pl.semaphore_signal(barrier, inc=1, device_id=align_device(me, 0), device_id_type=MESH)
        pl.semaphore_wait(barrier, len(near) + 4)

    @pl.when(me.band == me.z)
    def _():
        pl.semaphore_wait(barrier, len(near) + 3)


def align_device(me, step):
    return (me.z, me.half * 16 + me.band * 4 + (me.y + step) % 4)


class Tree:
    def __init__(self, me, mail, full, half, first):
        self.me, self.mail, self.full, self.half = me, mail, full, half
        self.first = first
        self.box = {}

    def off(self, f, s):
        return dict(dy=f % 4, dz=s % 4) if self.first == "y" else dict(dy=s % 4, dz=f % 4)

    def ref(self, f, s, part=None):
        return planes(self.full, self.me.piece(self.half, **self.off(f, s)), part)

    def push(self, key, src, f, s, df, ds, part=None):
        dst = self.ref(f, s, part)
        self.box[key] = self.mail.send(dst if src is None else src, dst, self.me.device(**self.off(df, ds)))

    def take(self, key, f, s, part=None):
        self.mail.arrive(self.box[key], self.ref(f, s, part), self.me.device(**self.off(0, 0)))

    def start(self, src):
        for d in (1, -1):
            self.push(("f", d), src, 0, 0, d, 0)
        for d in (1, -1):
            self.push(("s", 0, d), src, 0, 0, 0, d)

    def row(self):
        for d in (1, -1):
            self.take(("f", d), -d, 0)
            part = 0 if d == 1 else 1
            self.push(("f2", d), None, -d, 0, d, 0, part)
            for e in (1, -1):
                self.push(("s", -d, e), None, -d, 0, 0, e)

    def column(self, f):
        for e in (1, -1):
            self.take(("s", f, e), f, -e)
            part = 0 if e == 1 else 1
            self.push(("s2", f, e), None, f, -e, 0, e, part)

    def far(self):
        for d in (1, -1):
            self.take(("f2", d), 2, 0, 0 if d == 1 else 1)
        for e in (1, -1):
            self.push(("s", 2, e), None, 2, 0, 0, e)

    def last(self, f):
        for e in (1, -1):
            self.take(("s2", f, e), f, 2, 0 if e == 1 else 1)


def split(v):
    high = v.astype(jnp.bfloat16)
    return high, (v - high.astype(jnp.float32)).astype(jnp.bfloat16)


def times(v, table):
    r = jnp.dot(jnp.concatenate(split(v), axis=1), table, preferred_element_type=jnp.float32)
    return r[:, :GRID] + r[:, GRID:]


def under(table, va, vb):
    (ha, la), (hb, lb) = split(va), split(vb)
    values = jnp.concatenate([jnp.concatenate([ha, hb], axis=1), jnp.concatenate([la, lb], axis=1)], axis=0)
    r = jnp.dot(table, values, preferred_element_type=jnp.float32)
    r = r[:GRID] + r[GRID:]
    return r[:, :GRID], r[:, GRID:]


def gather(me, mail, res_ref, blk_ref, rfull, sfull, local_sem, forward):
    send_sem, recv_sem = mail.send_sem, mail.recv_sem
    h = me.half
    mine = me.piece(h)

    def spiece(dx, flip, t):
        x = (me.x + dx) % 4
        core = 1 - me.core if flip else me.core
        return (x // 2) * 16 + ((x % 2) * 2 + core) * 4 + (me.y + t) % 4

    order = (0, 1, 3, 2)
    align_no = {}
    for t in order:
        number = mail.count
        mail.count += 1
        align_no[t] = number
        src = blk_ref.at[(me.y + t) % 4]
        dst = planes(sfull, mine)

        def remote(src=src, dst=dst, t=t, number=number):
            return pltpu.make_async_remote_copy(
                src_ref=src, dst_ref=dst, send_sem=send_sem.at[number], recv_sem=recv_sem.at[number],
                device_id=align_device(me, t), device_id_type=MESH)
        if t:
            copy = remote()
            copy.start()
            mail.sent.append(copy)
        else:
            @pl.when(me.band != me.z)
            def _():
                remote().start()

            @pl.when(me.band == me.z)
            def _():
                pltpu.make_async_copy(src, dst, local_sem.at[1]).start()
            zero = (remote, src, dst)
    swap = mail.send(res_ref.at[1 - h], planes(rfull, mine), me.device(dx=2))
    tree_a = Tree(me, mail, rfull, h, "y")
    tree_b = Tree(me, mail, rfull, 1 - h, "z")
    tree_a.start(res_ref.at[h])
    own = pltpu.make_async_copy(res_ref.at[h], planes(rfull, mine), local_sem.at[0])
    own.start()
    mail.arrive(swap, planes(rfull, me.piece(1 - h)), me.device(dx=2))
    tree_b.start(None)

    xs = {}
    for t in order:
        back = -t % 4
        dst = planes(sfull, spiece(0, False, back))
        if t:
            mail.arrive(align_no[t], dst, align_device(me, back))
        else:
            @pl.when(me.band != me.z)
            def _():
                zero[0]().wait_recv()

            @pl.when(me.band == me.z)
            def _():
                pltpu.make_async_copy(zero[1], zero[2], local_sem.at[1]).wait()
        for d in (1, -1):
            xs[("x", d, back)] = mail.send(dst, dst, me.device(dx=d))
        xs[("c", 0, back)] = mail.send(dst, dst, me.device(flip=True))
    backs = [-t % 4 for t in order]
    tree_a.row()
    tree_b.row()
    tree_a.column(0)
    tree_b.column(0)
    for t in backs:
        for d in (1, -1):
            ref = planes(sfull, spiece(-d, False, t))
            mail.arrive(xs[("x", d, t)], ref, me.device(dx=-d))
            part = 0 if d == 1 else 1
            ref2 = planes(sfull, spiece(-d, False, t), part)
            xs[("x2", d, t)] = mail.send(ref2, ref2, me.device(dx=d))
            xs[("c", -d, t)] = mail.send(ref, ref, me.device(flip=True))
    tree_a.far()
    tree_b.far()
    for d in (-1, 1):
        tree_a.column(d)
        tree_b.column(d)
    for t in backs:
        for d in (1, -1):
            ref2 = planes(sfull, spiece(2, False, t), 0 if d == 1 else 1)
            mail.arrive(xs[("x2", d, t)], ref2, me.device(dx=-d))
        ref = planes(sfull, spiece(2, False, t))
        xs[("c", 2, t)] = mail.send(ref, ref, me.device(flip=True))
    tree_a.column(2)
    tree_b.column(2)
    for f in (0, -1, 1, 2):
        tree_a.last(f)
        tree_b.last(f)
    own.wait()
    for dx in (0, -1, 1, 2):
        forward([spiece(dx, False, t) for t in backs])
    for dx in (0, -1, 1, 2):
        for t in backs:
            mail.arrive(xs[("c", dx, t)], planes(sfull, spiece(dx, True, t)), me.device(flip=True))
        forward([spiece(dx, True, t) for t in backs])

    def finish():
        @pl.when(me.band != me.z)
        def _():
            zero[0]().wait_send()

    return finish


class Sum:
    def __init__(self, me, mail, term, near_s, far_s, near_f, far_f, half, first):
        self.me, self.mail, self.term = me, mail, term
        self.near_s, self.far_s, self.near_f, self.far_f = near_s, far_s, near_f, far_f
        self.half, self.first = half, first
        self.box = {}

    def off(self, f, s):
        return dict(dy=f % 4, dz=s % 4) if self.first == "y" else dict(dy=s % 4, dz=f % 4)

    def ref(self, f, s, part=None):
        return planes(self.term, self.me.piece(self.half, **self.off(f, s)), part)

    def slots(self, d, f=None):
        n = 0 if d == 1 else 1
        if f is None:
            return self.far_f.at[n], self.near_f.at[n]
        return self.far_s.at[f % 4, n], self.near_s.at[f % 4, n]

    def post(self, key, src, dst, df, ds):
        self.box[key] = self.mail.send(src, dst, self.me.device(**self.off(df, ds)))

    def add(self, key, into, slot):
        self.mail.arrive(self.box[key], slot, self.me.device())
        into[...] += slot[...]

    def far_column(self, f):
        for e in (1, -1):
            self.post(("a", f, e), self.ref(f, 2, 0 if e == 1 else 1), self.slots(e, f)[0], 0, e)

    def near_column(self, f):
        for e in (1, -1):
            self.add(("a", f, e), self.ref(f, e, 0 if e == 1 else 1), self.slots(e, f)[0])
            self.post(("b", f, e), self.ref(f, e), self.slots(e, f)[1], 0, e)

    def own_column(self, f):
        for e in (1, -1):
            self.add(("b", f, e), self.ref(f, 0), self.slots(e, f)[1])

    def far_row(self):
        for d in (1, -1):
            self.post(("c", d), self.ref(2, 0, 0 if d == 1 else 1), self.slots(d)[0], d, 0)

    def near_row(self, d):
        self.add(("c", d), self.ref(d, 0, 0 if d == 1 else 1), self.slots(d)[0])
        self.post(("d", d), self.ref(d, 0), self.slots(d)[1], d, 0)

    def own_row(self):
        for d in (1, -1):
            self.add(("d", d), self.ref(0, 0), self.slots(d)[1])


def kernel(res_ref, blk_ref, occ_ref, right_ref, right_t_ref, left_ref, left_t_ref, out_ref,
           rfull, sfull, work, near_s, far_s, near_f, far_f, send_sem, recv_sem, local_sem):
    me = Place()
    greet(me)
    mail = Mail(send_sem, recv_sem)
    h = me.half
    weight = -occ_ref[me.z * 4 + me.y]

    def forward(pieces):
        for piece in pieces:
            @pl.loop(0, PLANES // 2)
            def _(n):
                rows = pl.ds(pl.multiple_of(piece * ROWS + n * 2 * GRID, 2 * GRID), 2 * GRID)
                v = times(rfull[rows, :] * sfull[rows, :], right_ref[...])
                va, vb = under(left_t_ref[...], v[:GRID], v[GRID:])
                work[rows, :] = jnp.concatenate([va, vb], axis=0)

    def backward(pieces):
        for piece in pieces:
            @pl.loop(0, PLANES // 2)
            def _(n):
                start = pl.multiple_of(piece * ROWS + n * 2 * GRID, 2 * GRID)
                rows = pl.ds(start, 2 * GRID)
                va, vb = under(left_ref[...], work[pl.ds(start, GRID), :], work[pl.ds(start + GRID, GRID), :])
                v = times(jnp.concatenate([va, vb], axis=0), right_t_ref[...])
                work[rows, :] = v * (sfull[rows, :] * weight)

    finish = gather(me, mail, res_ref, blk_ref, rfull, sfull, local_sem, forward)

    def wave_sq(index):
        signed = jnp.minimum(index, GRID - index).astype(jnp.float32) * (2.0 * math.pi / GRID)
        return signed * signed

    shape = (GRID, GRID)
    base = wave_sq(lax.broadcasted_iota(jnp.int32, shape, 0)) + wave_sq(lax.broadcasted_iota(jnp.int32, shape, 1)) + KAPPA_SQ

    @pl.loop(0, GRID // 2)
    def _(n):
        ia, ib = pl.ds(2 * n, GRID, stride=GRID), pl.ds(2 * n + 1, GRID, stride=GRID)
        va, vb = under(left_t_ref[...], work[ia, :], work[ib, :])
        va = va * (4.0 * math.pi / (base + wave_sq(2 * n)))
        vb = vb * (4.0 * math.pi / (base + wave_sq(2 * n + 1)))
        va, vb = under(left_ref[...], va, vb)
        work[ia, :] = va
        work[ib, :] = vb

    sums = [
        Sum(me, mail, work, near_s.at[n], far_s.at[n], near_f.at[n], far_f.at[n], half, first)
        for n, (half, first) in enumerate(((1 - h, "z"), (h, "y")))
    ]
    order = (2, 1, -1, 0)

    def pieces(s, f, off):
        return [me.piece(s.half, **s.off(f, off))]

    for f in order:
        for s in sums:
            backward(pieces(s, f, 2))
            s.far_column(f)
    for f in order:
        for s in sums:
            backward(pieces(s, f, 1) + pieces(s, f, -1))
            s.near_column(f)
    for f in order:
        for s in sums:
            backward(pieces(s, f, 0))
    for f in order:
        for s in sums:
            s.own_column(f)
        for s in sums:
            if f == 2:
                s.far_row()
            elif f:
                s.near_row(f)
    for s in sums:
        s.own_row()
    away = planes(work, me.piece(1 - h))
    swap = mail.send(away, out_ref.at[h], me.device(dx=2))
    out_ref[h] = planes(work, me.piece(h))[...]
    mail.arrive(swap, out_ref.at[1 - h], me.device(dx=2))
    mail.finish()
    finish()


MESSAGES = 77 + 41


def basis():
    points = np.arange(GRID)
    freqs = np.minimum(points, GRID - points)
    angles = 2.0 * np.pi * ((points[:, None] * freqs[None, :]) % GRID) / GRID
    table = np.where(points[None, :] > GRID // 2, np.sin(angles), np.cos(angles)) * np.sqrt(2.0 / GRID)
    table[:, 0] /= np.sqrt(2.0)
    table[:, GRID // 2] /= np.sqrt(2.0)
    return table


def tables():
    b = basis()

    def parts(t):
        high = t.astype(ml_dtypes.bfloat16)
        return high, (t - high.astype(np.float64)).astype(ml_dtypes.bfloat16)

    def right(t):
        high, low = parts(t)
        return np.block([[high, low], [high, np.zeros_like(low)]])

    def left(t):
        high, low = parts(t)
        return np.block([[high, high], [low, np.zeros_like(low)]])

    return [jnp.asarray(t) for t in (right(b), right(b.T), left(b), left(b.T))]


def per_device(resident, blocks, occupation):
    vmem = pl.BlockSpec(memory_space=pltpu.VMEM)
    hbm = pl.BlockSpec(memory_space=pl.ANY)
    full = pltpu.VMEM((GRID * GRID, GRID), jnp.float32)
    out = pl.pallas_call(
        kernel,
        out_shape=jax.ShapeDtypeStruct((2, ROWS, GRID), jnp.float32),
        in_specs=[hbm, hbm, pl.BlockSpec(memory_space=pltpu.SMEM)] + [vmem] * 4,
        out_specs=vmem,
        scratch_shapes=[
            full,
            full,
            full,
            pltpu.VMEM((2, 4, 2, ROWS, GRID), jnp.float32),
            pltpu.VMEM((2, 4, 2, HALF, GRID), jnp.float32),
            pltpu.VMEM((2, 2, ROWS, GRID), jnp.float32),
            pltpu.VMEM((2, 2, HALF, GRID), jnp.float32),
            pltpu.SemaphoreType.DMA((MESSAGES,)),
            pltpu.SemaphoreType.DMA((MESSAGES,)),
            pltpu.SemaphoreType.DMA((2,)),
        ],
        compiler_params=pltpu.CompilerParams(
            collective_id=0, has_side_effects=True, vmem_limit_bytes=48 * 2**20
        ),
        cost_estimate=pl.CostEstimate(flops=13 * 10**9, bytes_accessed=10**7, transcendentals=0),
        name="exchange",
    )(
        resident.reshape(2, ROWS, GRID),
        blocks.reshape(4, ROWS, GRID),
        occupation,
        *tables(),
    )
    return out.reshape(2, PLANES, GRID, GRID)


def solution(mesh):
    placed = (P("band", "slab", None, None), P("band", "slab", None, None), P())
    return jax.shard_map(
        per_device,
        mesh=mesh,
        in_specs=placed,
        out_specs=P("band", "slab", None, None),
        check_vma=False,
    )
```

```python
import math

import jax
import ml_dtypes
import numpy as np
import jax.numpy as jnp
from jax import lax
from jax.experimental import pallas as pl
from jax.experimental.pallas import tpu as pltpu
from jax.sharding import PartitionSpec as P

MESH = pl.DeviceIdType.MESH
PLANES = 4
GRID = 128
ROWS = PLANES * GRID
HALF = ROWS // 2
KAPPA_SQ = 0.01
DEEP = 8


class Place:
    def __init__(self):
        self.band = lax.axis_index("band")
        slab = lax.axis_index("slab")
        self.core = self.band % 2
        self.half = slab // 16
        self.z = (slab // 4) % 4
        self.y = slab % 4
        self.x = self.half * 2 + self.band // 2
        self.stays = jnp.logical_and(self.band == self.z, self.core == 0)

    def device(self, dx=0, dy=0, dz=0, flip=False):
        x, y, z = (self.x + dx) % 4, (self.y + dy) % 4, (self.z + dz) % 4
        core = 1 - self.core if flip else self.core
        return ((x % 2) * 2 + core, (x // 2) * 16 + z * 4 + y)

    def piece(self, half, dy=0, dz=0):
        return half * 16 + ((self.z + dz) % 4) * 4 + (self.y + dy) % 4


class Mail:
    def __init__(self, send_sem, recv_sem):
        self.send_sem, self.recv_sem = send_sem, recv_sem
        self.count = 0
        self.sent = []

    def send(self, src, dst, device):
        number = self.count
        self.count += 1
        copy = pltpu.make_async_remote_copy(
            src_ref=src,
            dst_ref=dst,
            send_sem=self.send_sem.at[number],
            recv_sem=self.recv_sem.at[number],
            device_id=device,
            device_id_type=MESH,
        )
        copy.start()
        self.sent.append(copy)
        return number

    def arrive(self, number, dst, device):
        pltpu.make_async_remote_copy(
            src_ref=dst,
            dst_ref=dst,
            send_sem=self.send_sem.at[number],
            recv_sem=self.recv_sem.at[number],
            device_id=device,
            device_id_type=MESH,
        ).wait_recv()

    def finish(self):
        for copy in self.sent:
            copy.wait_send()


def planes(ref, piece, part=None):
    if part is None:
        return ref.at[pl.ds(piece * ROWS, ROWS)]
    return ref.at[pl.ds(piece * ROWS + part * HALF, HALF)]


def greet(me):
    barrier = pltpu.get_barrier_semaphore()
    near = [me.device(dx=1), me.device(dx=3), me.device(dy=1), me.device(dy=3),
            me.device(dz=1), me.device(dz=3), me.device(dx=2), me.device(flip=True)]
    for other in near:
        pl.semaphore_signal(barrier, inc=1, device_id=other, device_id_type=MESH)
    for k in range(1, 4):
        for other in (align_to(me, k), align_from(me, k)):
            pl.semaphore_signal(barrier, inc=1, device_id=other, device_id_type=MESH)

    @pl.when(jnp.logical_not(me.stays))
    def _():
        for other in (align_to(me, 0), align_from(me, 0)):
            pl.semaphore_signal(barrier, inc=1, device_id=other, device_id_type=MESH)
        pl.semaphore_wait(barrier, len(near) + 8)

    @pl.when(me.stays)
    def _():
        pl.semaphore_wait(barrier, len(near) + 6)


def align_to(me, step):
    band = ((me.z // 2 + me.core) % 2) * 2 + me.z % 2
    return (band, me.half * 16 + me.band * 4 + (me.y + step) % 4)


def align_z(me, x, core):
    return ((x + me.z) % 2) * 2 + core


def align_from(me, step):
    return (me.z, me.half * 16 + align_z(me, me.x, me.core) * 4 + (me.y - step) % 4)


class Tree:
    def __init__(self, me, mail, full, half, first):
        self.me, self.mail, self.full, self.half = me, mail, full, half
        self.first = first
        self.box = {}

    def off(self, f, s):
        return dict(dy=f % 4, dz=s % 4) if self.first == "y" else dict(dy=s % 4, dz=f % 4)

    def ref(self, f, s, part=None):
        return planes(self.full, self.me.piece(self.half, **self.off(f, s)), part)

    def push(self, key, src, f, s, df, ds, part=None):
        dst = self.ref(f, s, part)
        self.box[key] = self.mail.send(dst if src is None else src, dst, self.me.device(**self.off(df, ds)))

    def take(self, key, f, s, part=None):
        self.mail.arrive(self.box[key], self.ref(f, s, part), self.me.device(**self.off(0, 0)))

    def start(self, src):
        for d in (1, -1):
            self.push(("f", d), src, 0, 0, d, 0)
        for d in (1, -1):
            self.push(("s", 0, d), src, 0, 0, 0, d)

    def row(self):
        for d in (1, -1):
            self.take(("f", d), -d, 0)
            part = 0 if d == 1 else 1
            self.push(("f2", d), None, -d, 0, d, 0, part)
            for e in (1, -1):
                self.push(("s", -d, e), None, -d, 0, 0, e)

    def column(self, f):
        for e in (1, -1):
            self.take(("s", f, e), f, -e)
            part = 0 if e == 1 else 1
            self.push(("s2", f, e), None, f, -e, 0, e, part)

    def far(self):
        for d in (1, -1):
            self.take(("f2", d), 2, 0, 0 if d == 1 else 1)
        for e in (1, -1):
            self.push(("s", 2, e), None, 2, 0, 0, e)

    def last(self, f):
        for e in (1, -1):
            self.take(("s2", f, e), f, 2, 0 if e == 1 else 1)


def split(v):
    high = v.astype(jnp.bfloat16)
    return high, (v - high.astype(jnp.float32)).astype(jnp.bfloat16)


def times(v, table):
    r = jnp.dot(jnp.concatenate(split(v), axis=1), table, preferred_element_type=jnp.float32)
    return r[:, :GRID] + r[:, GRID:]


def under(table, va, vb):
    (ha, la), (hb, lb) = split(va), split(vb)
    values = jnp.concatenate([jnp.concatenate([ha, hb], axis=1), jnp.concatenate([la, lb], axis=1)], axis=0)
    r = jnp.dot(table, values, preferred_element_type=jnp.float32)
    r = r[:GRID] + r[GRID:]
    return r[:, :GRID], r[:, GRID:]


def gather(me, mail, res_ref, blk_ref, rfull, sfull, local_sem, forward):
    send_sem, recv_sem = mail.send_sem, mail.recv_sem
    h = me.half
    mine = me.piece(h)

    def spiece(dx, flip, t):
        x = (me.x + dx) % 4
        core = 1 - me.core if flip else me.core
        return (x // 2) * 16 + align_z(me, x, core) * 4 + (me.y + t) % 4

    order = (0, 1, 3, 2)
    align_no = {}
    for t in order:
        number = mail.count
        mail.count += 1
        align_no[t] = number
        src = blk_ref.at[(me.y + t) % 4]
        dst = planes(sfull, mine)

        def remote(src=src, dst=dst, t=t, number=number):
            return pltpu.make_async_remote_copy(
                src_ref=src, dst_ref=dst, send_sem=send_sem.at[number], recv_sem=recv_sem.at[number],
                device_id=align_to(me, t), device_id_type=MESH)
        if t:
            copy = remote()
            copy.start()
            mail.sent.append(copy)
        else:
            @pl.when(jnp.logical_not(me.stays))
            def _():
                remote().start()

            @pl.when(me.stays)
            def _():
                pltpu.make_async_copy(src, dst, local_sem.at[1]).start()
            zero = (remote, src, dst)
    swap = mail.send(res_ref.at[1 - h], planes(rfull, mine), me.device(dx=2))
    tree_a = Tree(me, mail, rfull, h, "y")
    tree_b = Tree(me, mail, rfull, 1 - h, "z")
    tree_a.start(res_ref.at[h])
    own = pltpu.make_async_copy(res_ref.at[h], planes(rfull, mine), local_sem.at[0])
    own.start()
    mail.arrive(swap, planes(rfull, me.piece(1 - h)), me.device(dx=2))
    tree_b.start(None)

    xs = {}
    for t in order:
        back = -t % 4
        dst = planes(sfull, spiece(0, False, back))
        if t:
            mail.arrive(align_no[t], dst, align_from(me, t))
        else:
            @pl.when(jnp.logical_not(me.stays))
            def _():
                zero[0]().wait_recv()

            @pl.when(me.stays)
            def _():
                pltpu.make_async_copy(zero[1], zero[2], local_sem.at[1]).wait()
        for d in (1, -1):
            xs[("x", d, back)] = mail.send(dst, dst, me.device(dx=d))
        xs[("c", 0, back)] = mail.send(dst, dst, me.device(flip=True))
    backs = [-t % 4 for t in order]
    tree_a.row()
    tree_b.row()
    tree_a.column(0)
    tree_b.column(0)
    for t in backs:
        for d in (1, -1):
            ref = planes(sfull, spiece(-d, False, t))
            mail.arrive(xs[("x", d, t)], ref, me.device(dx=-d))
            part = 0 if d == 1 else 1
            ref2 = planes(sfull, spiece(-d, False, t), part)
            xs[("x2", d, t)] = mail.send(ref2, ref2, me.device(dx=d))
            xs[("c", -d, t)] = mail.send(ref, ref, me.device(flip=True))
    tree_a.far()
    tree_b.far()
    for d in (-1, 1):
        tree_a.column(d)
        tree_b.column(d)
    for t in backs:
        for d in (1, -1):
            ref2 = planes(sfull, spiece(2, False, t), 0 if d == 1 else 1)
            mail.arrive(xs[("x2", d, t)], ref2, me.device(dx=-d))
        ref = planes(sfull, spiece(2, False, t))
        xs[("c", 2, t)] = mail.send(ref, ref, me.device(flip=True))
    tree_a.column(2)
    tree_b.column(2)
    for f in (0, -1, 1, 2):
        tree_a.last(f)
        tree_b.last(f)
    own.wait()
    for dx in (0, -1, 1, 2):
        forward([spiece(dx, False, t) for t in backs])
    for dx in (0, -1, 1, 2):
        for t in backs:
            mail.arrive(xs[("c", dx, t)], planes(sfull, spiece(dx, True, t)), me.device(flip=True))
        forward([spiece(dx, True, t) for t in backs])

    def finish():
        @pl.when(jnp.logical_not(me.stays))
        def _():
            zero[0]().wait_send()

    return finish


class Sum:
    def __init__(self, me, mail, term, near_s, far_s, near_f, far_f, half, first):
        self.me, self.mail, self.term = me, mail, term
        self.near_s, self.far_s, self.near_f, self.far_f = near_s, far_s, near_f, far_f
        self.half, self.first = half, first
        self.box = {}

    def off(self, f, s):
        return dict(dy=f % 4, dz=s % 4) if self.first == "y" else dict(dy=s % 4, dz=f % 4)

    def ref(self, f, s, part=None):
        return planes(self.term, self.me.piece(self.half, **self.off(f, s)), part)

    def slots(self, d, f=None):
        n = 0 if d == 1 else 1
        if f is None:
            return self.far_f.at[n], self.near_f.at[n]
        return self.far_s.at[f % 4, n], self.near_s.at[f % 4, n]

    def post(self, key, src, dst, df, ds):
        self.box[key] = self.mail.send(src, dst, self.me.device(**self.off(df, ds)))

    def add(self, key, into, slot):
        self.mail.arrive(self.box[key], slot, self.me.device())
        into[...] += slot[...]

    def far_column(self, f):
        for e in (1, -1):
            self.post(("a", f, e), self.ref(f, 2, 0 if e == 1 else 1), self.slots(e, f)[0], 0, e)

    def near_column(self, f):
        for e in (1, -1):
            self.add(("a", f, e), self.ref(f, e, 0 if e == 1 else 1), self.slots(e, f)[0])
            self.post(("b", f, e), self.ref(f, e), self.slots(e, f)[1], 0, e)

    def own_column(self, f):
        for e in (1, -1):
            self.add(("b", f, e), self.ref(f, 0), self.slots(e, f)[1])

    def far_row(self):
        for d in (1, -1):
            self.post(("c", d), self.ref(2, 0, 0 if d == 1 else 1), self.slots(d)[0], d, 0)

    def near_row(self, d):
        self.add(("c", d), self.ref(d, 0, 0 if d == 1 else 1), self.slots(d)[0])
        self.post(("d", d), self.ref(d, 0), self.slots(d)[1], d, 0)

    def own_row(self):
        for d in (1, -1):
            self.add(("d", d), self.ref(0, 0), self.slots(d)[1])


def kernel(res_ref, blk_ref, occ_ref, right_ref, right_t_ref, left_ref, left_t_ref, out_ref,
           rfull, sfull, work, near_s, far_s, near_f, far_f, send_sem, recv_sem, local_sem):
    me = Place()
    greet(me)
    mail = Mail(send_sem, recv_sem)
    h = me.half
    weight = -occ_ref[me.z * 4 + me.y]

    def units(pieces, n):
        return [pl.multiple_of(piece * ROWS + n * 2 * GRID, 2 * GRID) for piece in pieces]

    def forward(pieces):
        @pl.loop(0, PLANES // 2)
        def _(n):
            for start in units(pieces, n):
                rows = pl.ds(start, 2 * GRID)
                v = times(rfull[rows, :] * sfull[rows, :], right_ref[...])
                va, vb = under(left_t_ref[...], v[:GRID], v[GRID:])
                work[pl.ds(start, GRID), :] = va
                work[pl.ds(start + GRID, GRID), :] = vb

    def backward(pieces):
        @pl.loop(0, PLANES // 2)
        def _(n):
            starts = units(pieces, n)
            held = [work[pl.ds(start, 2 * GRID), :] for start in starts]
            results = []
            for start, v in zip(starts, held):
                va, vb = under(left_ref[...], v[:GRID], v[GRID:])
                v = times(jnp.concatenate([va, vb], axis=0), right_t_ref[...])
                results.append(v * (sfull[pl.ds(start, 2 * GRID), :] * weight))
            for start, v in zip(starts, results):
                work[pl.ds(start, 2 * GRID), :] = v

    finish = gather(me, mail, res_ref, blk_ref, rfull, sfull, local_sem, forward)

    def wave_sq(index):
        signed = jnp.minimum(index, GRID - index).astype(jnp.float32) * (2.0 * math.pi / GRID)
        return signed * signed

    shape = (GRID, GRID)
    base = wave_sq(lax.broadcasted_iota(jnp.int32, shape, 0)) + wave_sq(lax.broadcasted_iota(jnp.int32, shape, 1)) + KAPPA_SQ

    @pl.loop(0, GRID // (2 * DEEP))
    def _(n):
        indices = [(n * 2 * DEEP + 2 * k, n * 2 * DEEP + 2 * k + 1) for k in range(DEEP)]
        held = [[work[pl.ds(i, GRID, stride=GRID), :] for i in pair] for pair in indices]
        results = []
        for pair, values in zip(indices, held):
            values = under(left_t_ref[...], *values)
            values = [v * (4.0 * math.pi / (base + wave_sq(i))) for i, v in zip(pair, values)]
            results.append(under(left_ref[...], *values))
        for pair, values in zip(indices, results):
            for i, v in zip(pair, values):
                work[pl.ds(i, GRID, stride=GRID), :] = v

    sums = [
        Sum(me, mail, work, near_s.at[n], far_s.at[n], near_f.at[n], far_f.at[n], half, first)
        for n, (half, first) in enumerate(((1 - h, "z"), (h, "y")))
    ]
    order = (2, 1, -1, 0)

    def pieces(s, f, off):
        return [me.piece(s.half, **s.off(f, off))]

    for f in order:
        backward([p for s in sums for p in pieces(s, f, 2)])
        for s in sums:
            s.far_column(f)
    for f in order:
        backward([p for s in sums for e in (1, -1) for p in pieces(s, f, e)])
        for s in sums:
            s.near_column(f)
    for f in order:
        backward([p for s in sums for p in pieces(s, f, 0)])
    for f in order:
        for s in sums:
            s.own_column(f)
        for s in sums:
            if f == 2:
                s.far_row()
            elif f:
                s.near_row(f)
    for s in sums:
        s.own_row()
    away = planes(work, me.piece(1 - h))
    swap = mail.send(away, out_ref.at[h], me.device(dx=2))
    out_ref[h] = planes(work, me.piece(h))[...]
    mail.arrive(swap, out_ref.at[1 - h], me.device(dx=2))
    mail.finish()
    finish()


MESSAGES = 77 + 41


def basis():
    points = np.arange(GRID)
    freqs = np.minimum(points, GRID - points)
    angles = 2.0 * np.pi * ((points[:, None] * freqs[None, :]) % GRID) / GRID
    table = np.where(points[None, :] > GRID // 2, np.sin(angles), np.cos(angles)) * np.sqrt(2.0 / GRID)
    table[:, 0] /= np.sqrt(2.0)
    table[:, GRID // 2] /= np.sqrt(2.0)
    return table


def tables():
    b = basis()

    def parts(t):
        high = t.astype(ml_dtypes.bfloat16)
        return high, (t - high.astype(np.float64)).astype(ml_dtypes.bfloat16)

    def right(t):
        high, low = parts(t)
        return np.block([[high, low], [high, np.zeros_like(low)]])

    def left(t):
        high, low = parts(t)
        return np.block([[high, high], [low, np.zeros_like(low)]])

    return [jnp.asarray(t) for t in (right(b), right(b.T), left(b), left(b.T))]


def per_device(resident, blocks, occupation):
    vmem = pl.BlockSpec(memory_space=pltpu.VMEM)
    hbm = pl.BlockSpec(memory_space=pl.ANY)
    full = pltpu.VMEM((GRID * GRID, GRID), jnp.float32)
    out = pl.pallas_call(
        kernel,
        out_shape=jax.ShapeDtypeStruct((2, ROWS, GRID), jnp.float32),
        in_specs=[hbm, hbm, pl.BlockSpec(memory_space=pltpu.SMEM)] + [vmem] * 4,
        out_specs=vmem,
        scratch_shapes=[
            full,
            full,
            full,
            pltpu.VMEM((2, 4, 2, ROWS, GRID), jnp.float32),
            pltpu.VMEM((2, 4, 2, HALF, GRID), jnp.float32),
            pltpu.VMEM((2, 2, ROWS, GRID), jnp.float32),
            pltpu.VMEM((2, 2, HALF, GRID), jnp.float32),
            pltpu.SemaphoreType.DMA((MESSAGES,)),
            pltpu.SemaphoreType.DMA((MESSAGES,)),
            pltpu.SemaphoreType.DMA((2,)),
        ],
        compiler_params=pltpu.CompilerParams(
            collective_id=0, has_side_effects=True, vmem_limit_bytes=48 * 2**20
        ),
        cost_estimate=pl.CostEstimate(flops=13 * 10**9, bytes_accessed=10**7, transcendentals=0),
        name="exchange",
    )(
        resident.reshape(2, ROWS, GRID),
        blocks.reshape(4, ROWS, GRID),
        occupation,
        *tables(),
    )
    return out.reshape(2, PLANES, GRID, GRID)


def solution(mesh):
    placed = (P("band", "slab", None, None), P("band", "slab", None, None), P())
    return jax.shard_map(
        per_device,
        mesh=mesh,
        in_specs=placed,
        out_specs=P("band", "slab", None, None),
        check_vma=False,
    )
```

```python
import math

import jax
import ml_dtypes
import numpy as np
import jax.numpy as jnp
from jax import lax
from jax.experimental import pallas as pl
from jax.experimental.pallas import tpu as pltpu
from jax.sharding import PartitionSpec as P

MESH = pl.DeviceIdType.MESH
PLANES = 4
GRID = 128
ROWS = PLANES * GRID
HALF = ROWS // 2
KAPPA_SQ = 0.01
STEPS = ('s0', 'row', 'c0', 's1', 'far', 'c1', 's2', 'c2', 'own', 'early', 'last')
PITCH = GRID + 8
DEEP = 16


class Place:
    def __init__(self):
        self.band = lax.axis_index("band")
        slab = lax.axis_index("slab")
        self.core = self.band % 2
        self.half = slab // 16
        self.z = (slab // 4) % 4
        self.y = slab % 4
        self.x = self.half * 2 + self.band // 2
        self.stays = jnp.logical_and(self.band == self.z, self.core == 0)

    def device(self, dx=0, dy=0, dz=0, flip=False):
        x, y, z = (self.x + dx) % 4, (self.y + dy) % 4, (self.z + dz) % 4
        core = 1 - self.core if flip else self.core
        return ((x % 2) * 2 + core, (x // 2) * 16 + z * 4 + y)

    def piece(self, half, dy=0, dz=0):
        return half * 16 + ((self.z + dz) % 4) * 4 + (self.y + dy) % 4


class Mail:
    def __init__(self, send_sem, recv_sem):
        self.send_sem, self.recv_sem = send_sem, recv_sem
        self.count = 0
        self.sent = []

    def send(self, src, dst, device):
        number = self.count
        self.count += 1
        copy = pltpu.make_async_remote_copy(
            src_ref=src,
            dst_ref=dst,
            send_sem=self.send_sem.at[number],
            recv_sem=self.recv_sem.at[number],
            device_id=device,
            device_id_type=MESH,
        )
        copy.start()
        self.sent.append(copy)
        return number

    def arrive(self, number, dst, device):
        pltpu.make_async_remote_copy(
            src_ref=dst,
            dst_ref=dst,
            send_sem=self.send_sem.at[number],
            recv_sem=self.recv_sem.at[number],
            device_id=device,
            device_id_type=MESH,
        ).wait_recv()

    def finish(self):
        for copy in self.sent:
            copy.wait_send()


def planes(ref, piece, part=None):
    if part is None:
        return ref.at[pl.ds(piece * ROWS, ROWS)]
    return ref.at[pl.ds(piece * ROWS + part * HALF, HALF)]


def greet(me):
    barrier = pltpu.get_barrier_semaphore()
    near = [me.device(dx=1), me.device(dx=3), me.device(dy=1), me.device(dy=3),
            me.device(dz=1), me.device(dz=3), me.device(dx=2), me.device(flip=True)]
    for other in near:
        pl.semaphore_signal(barrier, inc=1, device_id=other, device_id_type=MESH)
    for k in range(1, 4):
        for other in (align_to(me, k), align_from(me, k)):
            pl.semaphore_signal(barrier, inc=1, device_id=other, device_id_type=MESH)

    @pl.when(jnp.logical_not(me.stays))
    def _():
        for other in (align_to(me, 0), align_from(me, 0)):
            pl.semaphore_signal(barrier, inc=1, device_id=other, device_id_type=MESH)
        pl.semaphore_wait(barrier, len(near) + 8)

    @pl.when(me.stays)
    def _():
        pl.semaphore_wait(barrier, len(near) + 6)


def align_to(me, step):
    band = ((me.z // 2 + me.core) % 2) * 2 + me.z % 2
    return (band, me.half * 16 + me.band * 4 + (me.y + step) % 4)


def align_z(me, x, core):
    return ((x + me.z) % 2) * 2 + core


def align_from(me, step):
    return (me.z, me.half * 16 + align_z(me, me.x, me.core) * 4 + (me.y - step) % 4)


class Tree:
    def __init__(self, me, mail, full, half, first):
        self.me, self.mail, self.full, self.half = me, mail, full, half
        self.first = first
        self.box = {}

    def off(self, f, s):
        return dict(dy=f % 4, dz=s % 4) if self.first == "y" else dict(dy=s % 4, dz=f % 4)

    def ref(self, f, s, part=None):
        return planes(self.full, self.me.piece(self.half, **self.off(f, s)), part)

    def push(self, key, src, f, s, df, ds, part=None):
        dst = self.ref(f, s, part)
        self.box[key] = self.mail.send(dst if src is None else src, dst, self.me.device(**self.off(df, ds)))

    def take(self, key, f, s, part=None):
        self.mail.arrive(self.box[key], self.ref(f, s, part), self.me.device(**self.off(0, 0)))

    def start(self, src):
        for d in (1, -1):
            self.push(("f", d), src, 0, 0, d, 0)
        for d in (1, -1):
            self.push(("s", 0, d), src, 0, 0, 0, d)

    def row(self):
        for d in (1, -1):
            self.take(("f", d), -d, 0)
            part = 0 if d == 1 else 1
            self.push(("f2", d), None, -d, 0, d, 0, part)
            for e in (1, -1):
                self.push(("s", -d, e), None, -d, 0, 0, e)

    def column(self, f):
        for e in (1, -1):
            self.take(("s", f, e), f, -e)
            part = 0 if e == 1 else 1
            self.push(("s2", f, e), None, f, -e, 0, e, part)

    def far(self):
        for d in (1, -1):
            self.take(("f2", d), 2, 0, 0 if d == 1 else 1)
        for e in (1, -1):
            self.push(("s", 2, e), None, 2, 0, 0, e)

    def last(self, f):
        for e in (1, -1):
            self.take(("s2", f, e), f, 2, 0 if e == 1 else 1)


def split(v):
    high = v.astype(jnp.bfloat16)
    return high, (v - high.astype(jnp.float32)).astype(jnp.bfloat16)


def times(v, table):
    r = jnp.dot(jnp.concatenate(split(v), axis=1), table, preferred_element_type=jnp.float32)
    return r[:, :GRID] + r[:, GRID:]


def under(table, va, vb):
    (ha, la), (hb, lb) = split(va), split(vb)
    values = jnp.concatenate([jnp.concatenate([ha, hb], axis=1), jnp.concatenate([la, lb], axis=1)], axis=0)
    r = jnp.dot(table, values, preferred_element_type=jnp.float32)
    r = r[:GRID] + r[GRID:]
    return r[:, :GRID], r[:, GRID:]


def gather(me, mail, res_ref, blk_ref, rfull, sfull, local_sem, forward):
    send_sem, recv_sem = mail.send_sem, mail.recv_sem
    h = me.half
    mine = me.piece(h)

    def spiece(dx, flip, t):
        x = (me.x + dx) % 4
        core = 1 - me.core if flip else me.core
        return (x // 2) * 16 + align_z(me, x, core) * 4 + (me.y + t) % 4

    order = (0, 1, 3, 2)
    align_no = {}
    for t in order:
        number = mail.count
        mail.count += 1
        align_no[t] = number
        src = blk_ref.at[(me.y + t) % 4]
        dst = planes(sfull, mine)

        def remote(src=src, dst=dst, t=t, number=number):
            return pltpu.make_async_remote_copy(
                src_ref=src, dst_ref=dst, send_sem=send_sem.at[number], recv_sem=recv_sem.at[number],
                device_id=align_to(me, t), device_id_type=MESH)
        if t:
            copy = remote()
            copy.start()
            mail.sent.append(copy)
        else:
            @pl.when(jnp.logical_not(me.stays))
            def _():
                remote().start()

            @pl.when(me.stays)
            def _():
                pltpu.make_async_copy(src, dst, local_sem.at[1]).start()
            zero = (remote, src, dst)
    swap = mail.send(res_ref.at[1 - h], planes(rfull, mine), me.device(dx=2))
    tree_a = Tree(me, mail, rfull, h, "y")
    tree_b = Tree(me, mail, rfull, 1 - h, "z")
    tree_a.start(res_ref.at[h])
    own = pltpu.make_async_copy(res_ref.at[h], planes(rfull, mine), local_sem.at[0])
    own.start()
    mail.arrive(swap, planes(rfull, me.piece(1 - h)), me.device(dx=2))
    tree_b.start(None)

    xs = {}
    backs = [-t % 4 for t in order]
    trees = (tree_a, tree_b)

    def collected():
        for t in order:
            back = -t % 4
            dst = planes(sfull, spiece(0, False, back))
            if t:
                mail.arrive(align_no[t], dst, align_from(me, t))
            else:
                @pl.when(jnp.logical_not(me.stays))
                def _():
                    zero[0]().wait_recv()

                @pl.when(me.stays)
                def _():
                    pltpu.make_async_copy(zero[1], zero[2], local_sem.at[1]).wait()
            for d in (1, -1):
                xs[("x", d, back)] = mail.send(dst, dst, me.device(dx=d))
            xs[("c", 0, back)] = mail.send(dst, dst, me.device(flip=True))

    def beside():
        for t in backs:
            for d in (1, -1):
                ref = planes(sfull, spiece(-d, False, t))
                mail.arrive(xs[("x", d, t)], ref, me.device(dx=-d))
                part = 0 if d == 1 else 1
                ref2 = planes(sfull, spiece(-d, False, t), part)
                xs[("x2", d, t)] = mail.send(ref2, ref2, me.device(dx=d))
                xs[("c", -d, t)] = mail.send(ref, ref, me.device(flip=True))

    def across():
        for t in backs:
            for d in (1, -1):
                ref2 = planes(sfull, spiece(2, False, t), 0 if d == 1 else 1)
                mail.arrive(xs[("x2", d, t)], ref2, me.device(dx=-d))
            ref = planes(sfull, spiece(2, False, t))
            xs[("c", 2, t)] = mail.send(ref, ref, me.device(flip=True))

    def column(*offsets):
        for f in offsets:
            for tree in trees:
                tree.column(f)

    def ready(late):
        for dx in (0, -1, 1, 2):
            x = (me.x + dx) % 4
            same = x // 2 == h
            close = align_z(me, x, me.core) != (me.z + 2) % 4
            whole = jnp.logical_and(same, jnp.logical_not(close) if late else close)

            @pl.when(whole)
            def _():
                forward([spiece(dx, False, t) for t in range(4)])

            @pl.when(jnp.logical_not(same))
            def _():
                forward([spiece(dx, False, t) for t in ((2,) if late else (0, 1, 3))])

    steps = {
        "own": own.wait,
        "row": lambda: [tree.row() for tree in trees],
        "far": lambda: [tree.far() for tree in trees],
        "c0": lambda: column(0),
        "c1": lambda: column(-1, 1),
        "c2": lambda: column(2),
        "last": lambda: [tree.last(f) for f in (0, -1, 1, 2) for tree in trees],
        "early": lambda: ready(False),
        "s0": collected,
        "s1": beside,
        "s2": across,
    }
    for step in STEPS:
        steps[step]()
    ready(True)
    for dx in (0, -1, 1, 2):
        for t in backs:
            mail.arrive(xs[("c", dx, t)], planes(sfull, spiece(dx, True, t)), me.device(flip=True))
        forward([spiece(dx, True, t) for t in backs])

    def finish():
        @pl.when(jnp.logical_not(me.stays))
        def _():
            zero[0]().wait_send()

    return finish


class Sum:
    def __init__(self, me, mail, term, near_s, far_s, near_f, far_f, half, first):
        self.me, self.mail, self.term = me, mail, term
        self.near_s, self.far_s, self.near_f, self.far_f = near_s, far_s, near_f, far_f
        self.half, self.first = half, first
        self.box = {}

    def off(self, f, s):
        return dict(dy=f % 4, dz=s % 4) if self.first == "y" else dict(dy=s % 4, dz=f % 4)

    def ref(self, f, s, part=None):
        return planes(self.term, self.me.piece(self.half, **self.off(f, s)), part)

    def slots(self, d, f=None):
        n = 0 if d == 1 else 1
        if f is None:
            return self.far_f.at[n], self.near_f.at[n]
        return self.far_s.at[f % 4, n], self.near_s.at[f % 4, n]

    def post(self, key, src, dst, df, ds):
        self.box[key] = self.mail.send(src, dst, self.me.device(**self.off(df, ds)))

    def add(self, key, into, slot):
        self.mail.arrive(self.box[key], slot, self.me.device())
        into[...] += slot[...]

    def far_column(self, f):
        for e in (1, -1):
            self.post(("a", f, e), self.ref(f, 2, 0 if e == 1 else 1), self.slots(e, f)[0], 0, e)

    def near_column(self, f):
        for e in (1, -1):
            self.add(("a", f, e), self.ref(f, e, 0 if e == 1 else 1), self.slots(e, f)[0])
            self.post(("b", f, e), self.ref(f, e), self.slots(e, f)[1], 0, e)

    def own_column(self, f):
        for e in (1, -1):
            self.add(("b", f, e), self.ref(f, 0), self.slots(e, f)[1])

    def far_row(self):
        for d in (1, -1):
            self.post(("c", d), self.ref(2, 0, 0 if d == 1 else 1), self.slots(d)[0], d, 0)

    def near_row(self, d):
        self.add(("c", d), self.ref(d, 0, 0 if d == 1 else 1), self.slots(d)[0])
        self.post(("d", d), self.ref(d, 0), self.slots(d)[1], d, 0)

    def own_row(self):
        for d in (1, -1):
            self.add(("d", d), self.ref(0, 0), self.slots(d)[1])


def kernel(res_ref, blk_ref, occ_ref, right_ref, right_t_ref, left_ref, left_t_ref, out_ref,
           rfull, sfull, term, work, near_s, far_s, near_f, far_f, send_sem, recv_sem, local_sem):
    me = Place()
    greet(me)
    mail = Mail(send_sem, recv_sem)
    h = me.half
    weight = -occ_ref[me.z * 4 + me.y]

    def units(pieces, n):
        return [pl.multiple_of(piece * ROWS + n * 2 * GRID, 2 * GRID) for piece in pieces]

    def pitched(start):
        first = pl.multiple_of(start // GRID * PITCH, 8)
        return pl.ds(first, GRID), pl.ds(pl.multiple_of(first + PITCH, 8), GRID)

    def forward(pieces):
        @pl.loop(0, PLANES // 2)
        def _(n):
            for start in units(pieces, n):
                rows = pl.ds(start, 2 * GRID)
                v = times(rfull[rows, :] * sfull[rows, :], right_ref[...])
                va, vb = under(left_t_ref[...], v[:GRID], v[GRID:])
                one, two = pitched(start)
                work[one, :] = va
                work[two, :] = vb

    def backward(pieces):
        @pl.loop(0, PLANES // 2)
        def _(n):
            starts = units(pieces, n)
            held = [[work[rows, :] for rows in pitched(start)] for start in starts]
            results = []
            for start, values in zip(starts, held):
                va, vb = under(left_ref[...], *values)
                v = times(jnp.concatenate([va, vb], axis=0), right_t_ref[...])
                results.append(v * (sfull[pl.ds(start, 2 * GRID), :] * weight))
            for start, v in zip(starts, results):
                term[pl.ds(start, 2 * GRID), :] = v

    finish = gather(me, mail, res_ref, blk_ref, rfull, sfull, local_sem, forward)

    def wave_sq(index):
        signed = jnp.minimum(index, GRID - index).astype(jnp.float32) * (2.0 * math.pi / GRID)
        return signed * signed

    shape = (GRID, GRID)
    base = wave_sq(lax.broadcasted_iota(jnp.int32, shape, 0)) + wave_sq(lax.broadcasted_iota(jnp.int32, shape, 1)) + KAPPA_SQ

    @pl.loop(0, GRID // (2 * DEEP))
    def _(n):
        indices = [(n * 2 * DEEP + 2 * k, n * 2 * DEEP + 2 * k + 1) for k in range(DEEP)]
        held = [[work[pl.ds(i, GRID, stride=PITCH), :] for i in pair] for pair in indices]
        results = []
        for pair, values in zip(indices, held):
            values = under(left_t_ref[...], *values)
            values = [v * (4.0 * math.pi / (base + wave_sq(i))) for i, v in zip(pair, values)]
            results.append(under(left_ref[...], *values))
        for pair, values in zip(indices, results):
            for i, v in zip(pair, values):
                work[pl.ds(i, GRID, stride=PITCH), :] = v

    sums = [
        Sum(me, mail, term, near_s.at[n], far_s.at[n], near_f.at[n], far_f.at[n], half, first)
        for n, (half, first) in enumerate(((1 - h, "z"), (h, "y")))
    ]
    order = (2, 1, -1, 0)

    def pieces(s, f, off):
        return [me.piece(s.half, **s.off(f, off))]

    for f in order:
        backward([p for s in sums for p in pieces(s, f, 2)])
        for s in sums:
            s.far_column(f)
    for f in order:
        backward([p for s in sums for e in (1, -1) for p in pieces(s, f, e)])
        for s in sums:
            s.near_column(f)
    for f in order:
        backward([p for s in sums for p in pieces(s, f, 0)])
    for f in order:
        for s in sums:
            s.own_column(f)
        for s in sums:
            if f == 2:
                s.far_row()
            elif f:
                s.near_row(f)
    sums[0].own_row()
    swap = mail.send(planes(term, me.piece(1 - h)), out_ref.at[h], me.device(dx=2))
    sums[1].own_row()
    mail.arrive(swap, out_ref.at[1 - h], me.device(dx=2))
    mail.finish()
    out_ref[h] = planes(term, me.piece(h))[...]
    finish()


MESSAGES = 77 + 41


def basis():
    points = np.arange(GRID)
    freqs = np.minimum(points, GRID - points)
    angles = 2.0 * np.pi * ((points[:, None] * freqs[None, :]) % GRID) / GRID
    table = np.where(points[None, :] > GRID // 2, np.sin(angles), np.cos(angles)) * np.sqrt(2.0 / GRID)
    table[:, 0] /= np.sqrt(2.0)
    table[:, GRID // 2] /= np.sqrt(2.0)
    return table


def tables():
    b = basis()

    def parts(t):
        high = t.astype(ml_dtypes.bfloat16)
        return high, (t - high.astype(np.float64)).astype(ml_dtypes.bfloat16)

    def right(t):
        high, low = parts(t)
        return np.block([[high, low], [high, np.zeros_like(low)]])

    def left(t):
        high, low = parts(t)
        return np.block([[high, high], [low, np.zeros_like(low)]])

    return [jnp.asarray(t) for t in (right(b), right(b.T), left(b), left(b.T))]


def per_device(resident, blocks, occupation):
    vmem = pl.BlockSpec(memory_space=pltpu.VMEM)
    hbm = pl.BlockSpec(memory_space=pl.ANY)
    full = pltpu.VMEM((GRID * GRID, GRID), jnp.float32)
    out = pl.pallas_call(
        kernel,
        out_shape=jax.ShapeDtypeStruct((2, ROWS, GRID), jnp.float32),
        in_specs=[hbm, hbm, pl.BlockSpec(memory_space=pltpu.SMEM)] + [vmem] * 4,
        out_specs=vmem,
        scratch_shapes=[
            full,
            full,
            full,
            pltpu.VMEM((GRID * PITCH, GRID), jnp.float32),
            pltpu.VMEM((2, 4, 2, ROWS, GRID), jnp.float32),
            pltpu.VMEM((2, 4, 2, HALF, GRID), jnp.float32),
            pltpu.VMEM((2, 2, ROWS, GRID), jnp.float32),
            pltpu.VMEM((2, 2, HALF, GRID), jnp.float32),
            pltpu.SemaphoreType.DMA((MESSAGES,)),
            pltpu.SemaphoreType.DMA((MESSAGES,)),
            pltpu.SemaphoreType.DMA((2,)),
        ],
        compiler_params=pltpu.CompilerParams(
            collective_id=0, has_side_effects=True, vmem_limit_bytes=56 * 2**20
        ),
        cost_estimate=pl.CostEstimate(flops=13 * 10**9, bytes_accessed=10**7, transcendentals=0),
        name="exchange",
    )(
        resident.reshape(2, ROWS, GRID),
        blocks.reshape(4, ROWS, GRID),
        occupation,
        *tables(),
    )
    return out.reshape(2, PLANES, GRID, GRID)


def solution(mesh):
    placed = (P("band", "slab", None, None), P("band", "slab", None, None), P())
    return jax.shard_map(
        per_device,
        mesh=mesh,
        in_specs=placed,
        out_specs=P("band", "slab", None, None),
        check_vma=False,
    )
```

```python
import math

import jax
import ml_dtypes
import numpy as np
import jax.numpy as jnp
from jax import lax
from jax.experimental import pallas as pl
from jax.experimental.pallas import tpu as pltpu
from jax.sharding import PartitionSpec as P

MESH = pl.DeviceIdType.MESH
PLANES = 4
GRID = 128
ROWS = PLANES * GRID
HALF = ROWS // 2
KAPPA_SQ = 0.01
STEPS = ('s0', 'row', 'c0', 's1', 'far', 'c1', 's2', 'c2', 'own', 'early', 'last')
PITCH = GRID + 8
DEEP = 16


class Place:
    def __init__(self):
        self.band = lax.axis_index("band")
        slab = lax.axis_index("slab")
        self.core = self.band % 2
        self.half = slab // 16
        self.z = (slab // 4) % 4
        self.y = slab % 4
        self.x = self.half * 2 + self.band // 2
        self.stays = jnp.logical_and(self.band == 0, self.z == 0)

    def device(self, dx=0, dy=0, dz=0, flip=False):
        x, y, z = (self.x + dx) % 4, (self.y + dy) % 4, (self.z + dz) % 4
        core = 1 - self.core if flip else self.core
        return ((x % 2) * 2 + core, (x // 2) * 16 + z * 4 + y)

    def piece(self, half, dy=0, dz=0):
        return half * 16 + ((self.z + dz) % 4) * 4 + (self.y + dy) % 4


class Mail:
    def __init__(self, send_sem, recv_sem):
        self.send_sem, self.recv_sem = send_sem, recv_sem
        self.count = 0
        self.sent = []

    def send(self, src, dst, device):
        number = self.count
        self.count += 1
        copy = pltpu.make_async_remote_copy(
            src_ref=src,
            dst_ref=dst,
            send_sem=self.send_sem.at[number],
            recv_sem=self.recv_sem.at[number],
            device_id=device,
            device_id_type=MESH,
        )
        copy.start()
        self.sent.append(copy)
        return number

    def arrive(self, number, dst, device):
        pltpu.make_async_remote_copy(
            src_ref=dst,
            dst_ref=dst,
            send_sem=self.send_sem.at[number],
            recv_sem=self.recv_sem.at[number],
            device_id=device,
            device_id_type=MESH,
        ).wait_recv()

    def finish(self):
        for copy in self.sent:
            copy.wait_send()


def planes(ref, piece, part=None):
    if part is None:
        return ref.at[pl.ds(piece * ROWS, ROWS)]
    return ref.at[pl.ds(piece * ROWS + part * HALF, HALF)]


def greet(me):
    barrier = pltpu.get_barrier_semaphore()
    near = [me.device(dx=1), me.device(dx=3), me.device(dy=1), me.device(dy=3),
            me.device(dz=1), me.device(dz=3), me.device(dx=2), me.device(flip=True)]
    for other in near:
        pl.semaphore_signal(barrier, inc=1, device_id=other, device_id_type=MESH)
    for k in range(1, 4):
        for other in (align_to(me, k), align_from(me, k)):
            pl.semaphore_signal(barrier, inc=1, device_id=other, device_id_type=MESH)

    @pl.when(jnp.logical_not(me.stays))
    def _():
        for other in (align_to(me, 0), align_from(me, 0)):
            pl.semaphore_signal(barrier, inc=1, device_id=other, device_id_type=MESH)
        pl.semaphore_wait(barrier, len(near) + 8)

    @pl.when(me.stays)
    def _():
        pl.semaphore_wait(barrier, len(near) + 6)


def align_to(me, step):
    band = ((me.band + me.z) % 2) * 2 + me.z // 2
    return (band, me.half * 16 + me.band * 4 + (me.y + step) % 4)


def align_z(me, x, core):
    return core * 2 + (x + me.z) % 2


def align_from(me, step):
    return (me.z, me.half * 16 + align_z(me, me.x, me.core) * 4 + (me.y - step) % 4)


class Tree:
    def __init__(self, me, mail, full, half, first):
        self.me, self.mail, self.full, self.half = me, mail, full, half
        self.first = first
        self.box = {}

    def off(self, f, s):
        return dict(dy=f % 4, dz=s % 4) if self.first == "y" else dict(dy=s % 4, dz=f % 4)

    def ref(self, f, s, part=None):
        return planes(self.full, self.me.piece(self.half, **self.off(f, s)), part)

    def push(self, key, src, f, s, df, ds, part=None):
        dst = self.ref(f, s, part)
        self.box[key] = self.mail.send(dst if src is None else src, dst, self.me.device(**self.off(df, ds)))

    def take(self, key, f, s, part=None):
        self.mail.arrive(self.box[key], self.ref(f, s, part), self.me.device(**self.off(0, 0)))

    def start(self, src):
        for d in (1, -1):
            self.push(("f", d), src, 0, 0, d, 0)
        for d in (1, -1):
            self.push(("s", 0, d), src, 0, 0, 0, d)

    def row(self):
        for d in (1, -1):
            self.take(("f", d), -d, 0)
            part = 0 if d == 1 else 1
            self.push(("f2", d), None, -d, 0, d, 0, part)
            for e in (1, -1):
                self.push(("s", -d, e), None, -d, 0, 0, e)

    def column(self, f):
        for e in (1, -1):
            self.take(("s", f, e), f, -e)
            part = 0 if e == 1 else 1
            self.push(("s2", f, e), None, f, -e, 0, e, part)

    def far(self):
        for d in (1, -1):
            self.take(("f2", d), 2, 0, 0 if d == 1 else 1)
        for e in (1, -1):
            self.push(("s", 2, e), None, 2, 0, 0, e)

    def last(self, f):
        for e in (1, -1):
            self.take(("s2", f, e), f, 2, 0 if e == 1 else 1)


def split(v):
    high = v.astype(jnp.bfloat16)
    return high, (v - high.astype(jnp.float32)).astype(jnp.bfloat16)


def times(v, table):
    r = jnp.dot(jnp.concatenate(split(v), axis=1), table, preferred_element_type=jnp.float32)
    return r[:, :GRID] + r[:, GRID:]


def under(table, va, vb):
    (ha, la), (hb, lb) = split(va), split(vb)
    values = jnp.concatenate([jnp.concatenate([ha, hb], axis=1), jnp.concatenate([la, lb], axis=1)], axis=0)
    r = jnp.dot(table, values, preferred_element_type=jnp.float32)
    r = r[:GRID] + r[GRID:]
    return r[:, :GRID], r[:, GRID:]


def gather(me, mail, res_ref, blk_ref, rfull, sfull, local_sem, forward):
    send_sem, recv_sem = mail.send_sem, mail.recv_sem
    h = me.half
    mine = me.piece(h)

    def spiece(dx, flip, t):
        x = (me.x + dx) % 4
        core = 1 - me.core if flip else me.core
        return (x // 2) * 16 + align_z(me, x, core) * 4 + (me.y + t) % 4

    order = (0, 1, 3, 2)
    align_no = {}
    for t in order:
        number = mail.count
        mail.count += 1
        align_no[t] = number
        src = blk_ref.at[(me.y + t) % 4]
        dst = planes(sfull, mine)

        def remote(src=src, dst=dst, t=t, number=number):
            return pltpu.make_async_remote_copy(
                src_ref=src, dst_ref=dst, send_sem=send_sem.at[number], recv_sem=recv_sem.at[number],
                device_id=align_to(me, t), device_id_type=MESH)
        if t:
            copy = remote()
            copy.start()
            mail.sent.append(copy)
        else:
            @pl.when(jnp.logical_not(me.stays))
            def _():
                remote().start()

            @pl.when(me.stays)
            def _():
                pltpu.make_async_copy(src, dst, local_sem.at[1]).start()
            zero = (remote, src, dst)
    swap = mail.send(res_ref.at[1 - h], planes(rfull, mine), me.device(dx=2))
    tree_a = Tree(me, mail, rfull, h, "y")
    tree_b = Tree(me, mail, rfull, 1 - h, "z")
    tree_a.start(res_ref.at[h])
    own = pltpu.make_async_copy(res_ref.at[h], planes(rfull, mine), local_sem.at[0])
    own.start()
    mail.arrive(swap, planes(rfull, me.piece(1 - h)), me.device(dx=2))
    tree_b.start(None)

    xs = {}
    backs = [-t % 4 for t in order]
    trees = (tree_a, tree_b)

    def collected():
        for t in order:
            back = -t % 4
            dst = planes(sfull, spiece(0, False, back))
            if t:
                mail.arrive(align_no[t], dst, align_from(me, t))
            else:
                @pl.when(jnp.logical_not(me.stays))
                def _():
                    zero[0]().wait_recv()

                @pl.when(me.stays)
                def _():
                    pltpu.make_async_copy(zero[1], zero[2], local_sem.at[1]).wait()
            for d in (1, -1):
                xs[("x", d, back)] = mail.send(dst, dst, me.device(dx=d))
            xs[("c", 0, back)] = mail.send(dst, dst, me.device(flip=True))

    def beside():
        for t in backs:
            for d in (1, -1):
                ref = planes(sfull, spiece(-d, False, t))
                mail.arrive(xs[("x", d, t)], ref, me.device(dx=-d))
                part = 0 if d == 1 else 1
                ref2 = planes(sfull, spiece(-d, False, t), part)
                xs[("x2", d, t)] = mail.send(ref2, ref2, me.device(dx=d))
                xs[("c", -d, t)] = mail.send(ref, ref, me.device(flip=True))

    def across():
        for t in backs:
            for d in (1, -1):
                ref2 = planes(sfull, spiece(2, False, t), 0 if d == 1 else 1)
                mail.arrive(xs[("x2", d, t)], ref2, me.device(dx=-d))
            ref = planes(sfull, spiece(2, False, t))
            xs[("c", 2, t)] = mail.send(ref, ref, me.device(flip=True))

    def column(*offsets):
        for f in offsets:
            for tree in trees:
                tree.column(f)

    def ready(late):
        for dx in (0, -1, 1, 2):
            x = (me.x + dx) % 4
            same = x // 2 == h
            close = align_z(me, x, me.core) != (me.z + 2) % 4
            whole = jnp.logical_and(same, jnp.logical_not(close) if late else close)

            @pl.when(whole)
            def _():
                forward([spiece(dx, False, t) for t in range(4)])

            @pl.when(jnp.logical_not(same))
            def _():
                forward([spiece(dx, False, t) for t in ((2,) if late else (0, 1, 3))])

    steps = {
        "own": own.wait,
        "row": lambda: [tree.row() for tree in trees],
        "far": lambda: [tree.far() for tree in trees],
        "c0": lambda: column(0),
        "c1": lambda: column(-1, 1),
        "c2": lambda: column(2),
        "last": lambda: [tree.last(f) for f in (0, -1, 1, 2) for tree in trees],
        "early": lambda: ready(False),
        "s0": collected,
        "s1": beside,
        "s2": across,
    }
    for step in STEPS:
        steps[step]()
    ready(True)
    for dx in (0, -1, 1, 2):
        for t in backs:
            mail.arrive(xs[("c", dx, t)], planes(sfull, spiece(dx, True, t)), me.device(flip=True))
        forward([spiece(dx, True, t) for t in backs])

    def finish():
        @pl.when(jnp.logical_not(me.stays))
        def _():
            zero[0]().wait_send()

    return finish


class Sum:
    def __init__(self, me, mail, term, near_s, far_s, near_f, far_f, half, first):
        self.me, self.mail, self.term = me, mail, term
        self.near_s, self.far_s, self.near_f, self.far_f = near_s, far_s, near_f, far_f
        self.half, self.first = half, first
        self.box = {}

    def off(self, f, s):
        return dict(dy=f % 4, dz=s % 4) if self.first == "y" else dict(dy=s % 4, dz=f % 4)

    def ref(self, f, s, part=None):
        return planes(self.term, self.me.piece(self.half, **self.off(f, s)), part)

    def slots(self, d, f=None):
        n = 0 if d == 1 else 1
        if f is None:
            return self.far_f.at[n], self.near_f.at[n]
        return self.far_s.at[f % 4, n], self.near_s.at[f % 4, n]

    def post(self, key, src, dst, df, ds):
        self.box[key] = self.mail.send(src, dst, self.me.device(**self.off(df, ds)))

    def add(self, key, into, slot):
        self.mail.arrive(self.box[key], slot, self.me.device())
        into[...] += slot[...]

    def far_column(self, f):
        for e in (1, -1):
            self.post(("a", f, e), self.ref(f, 2, 0 if e == 1 else 1), self.slots(e, f)[0], 0, e)

    def near_column(self, f):
        for e in (1, -1):
            self.add(("a", f, e), self.ref(f, e, 0 if e == 1 else 1), self.slots(e, f)[0])
            self.post(("b", f, e), self.ref(f, e), self.slots(e, f)[1], 0, e)

    def own_column(self, f):
        for e in (1, -1):
            self.add(("b", f, e), self.ref(f, 0), self.slots(e, f)[1])

    def far_row(self):
        for d in (1, -1):
            self.post(("c", d), self.ref(2, 0, 0 if d == 1 else 1), self.slots(d)[0], d, 0)

    def near_row(self, d):
        self.add(("c", d), self.ref(d, 0, 0 if d == 1 else 1), self.slots(d)[0])
        self.post(("d", d), self.ref(d, 0), self.slots(d)[1], d, 0)

    def own_row(self):
        for d in (1, -1):
            self.add(("d", d), self.ref(0, 0), self.slots(d)[1])


def kernel(res_ref, blk_ref, occ_ref, right_ref, right_t_ref, left_ref, left_t_ref, out_ref,
           rfull, sfull, term, work, near_s, far_s, near_f, far_f, send_sem, recv_sem, local_sem):
    me = Place()
    greet(me)
    mail = Mail(send_sem, recv_sem)
    h = me.half
    weight = -occ_ref[me.z * 4 + me.y]

    def units(pieces, n):
        return [pl.multiple_of(piece * ROWS + n * 2 * GRID, 2 * GRID) for piece in pieces]

    def pitched(start):
        first = pl.multiple_of(start // GRID * PITCH, 8)
        return pl.ds(first, GRID), pl.ds(pl.multiple_of(first + PITCH, 8), GRID)

    def forward(pieces):
        @pl.loop(0, PLANES // 2)
        def _(n):
            for start in units(pieces, n):
                rows = pl.ds(start, 2 * GRID)
                v = times(rfull[rows, :] * sfull[rows, :], right_ref[...])
                va, vb = under(left_t_ref[...], v[:GRID], v[GRID:])
                one, two = pitched(start)
                work[one, :] = va
                work[two, :] = vb

    def backward(pieces):
        @pl.loop(0, PLANES // 2)
        def _(n):
            starts = units(pieces, n)
            held = [[work[rows, :] for rows in pitched(start)] for start in starts]
            results = []
            for start, values in zip(starts, held):
                va, vb = under(left_ref[...], *values)
                v = times(jnp.concatenate([va, vb], axis=0), right_t_ref[...])
                results.append(v * (sfull[pl.ds(start, 2 * GRID), :] * weight))
            for start, v in zip(starts, results):
                term[pl.ds(start, 2 * GRID), :] = v

    finish = gather(me, mail, res_ref, blk_ref, rfull, sfull, local_sem, forward)

    def wave_sq(index):
        signed = jnp.minimum(index, GRID - index).astype(jnp.float32) * (2.0 * math.pi / GRID)
        return signed * signed

    shape = (GRID, GRID)
    base = wave_sq(lax.broadcasted_iota(jnp.int32, shape, 0)) + wave_sq(lax.broadcasted_iota(jnp.int32, shape, 1)) + KAPPA_SQ

    @pl.loop(0, GRID // (2 * DEEP))
    def _(n):
        indices = [(n * 2 * DEEP + 2 * k, n * 2 * DEEP + 2 * k + 1) for k in range(DEEP)]
        held = [[work[pl.ds(i, GRID, stride=PITCH), :] for i in pair] for pair in indices]
        results = []
        for pair, values in zip(indices, held):
            values = under(left_t_ref[...], *values)
            values = [v * (4.0 * math.pi / (base + wave_sq(i))) for i, v in zip(pair, values)]
            results.append(under(left_ref[...], *values))
        for pair, values in zip(indices, results):
            for i, v in zip(pair, values):
                work[pl.ds(i, GRID, stride=PITCH), :] = v

    sums = [
        Sum(me, mail, term, near_s.at[n], far_s.at[n], near_f.at[n], far_f.at[n], half, first)
        for n, (half, first) in enumerate(((1 - h, "z"), (h, "y")))
    ]
    order = (2, 1, -1, 0)

    def pieces(s, f, off):
        return [me.piece(s.half, **s.off(f, off))]

    for f in order:
        backward([p for s in sums for p in pieces(s, f, 2)])
        for s in sums:
            s.far_column(f)
    def near(f):
        backward([p for s in sums for e in (1, -1) for p in pieces(s, f, e)])
        for s in sums:
            s.near_column(f)

    def own(f):
        backward([p for s in sums for p in pieces(s, f, 0)])
        for s in sums:
            s.own_column(f)
        for s in sums:
            if f == 2:
                s.far_row()
            elif f:
                s.near_row(f)

    for step, f in ((near, 2), (near, 1), (near, -1), (own, 2), (near, 0), (own, 1), (own, -1), (own, 0)):
        step(f)
    sums[0].own_row()
    swap = mail.send(planes(term, me.piece(1 - h)), out_ref.at[h], me.device(dx=2))
    sums[1].own_row()
    mail.arrive(swap, out_ref.at[1 - h], me.device(dx=2))
    mail.finish()
    out_ref[h] = planes(term, me.piece(h))[...]
    finish()


MESSAGES = 77 + 41


def basis():
    points = np.arange(GRID)
    freqs = np.minimum(points, GRID - points)
    angles = 2.0 * np.pi * ((points[:, None] * freqs[None, :]) % GRID) / GRID
    table = np.where(points[None, :] > GRID // 2, np.sin(angles), np.cos(angles)) * np.sqrt(2.0 / GRID)
    table[:, 0] /= np.sqrt(2.0)
    table[:, GRID // 2] /= np.sqrt(2.0)
    return table


def tables():
    b = basis()

    def parts(t):
        high = t.astype(ml_dtypes.bfloat16)
        return high, (t - high.astype(np.float64)).astype(ml_dtypes.bfloat16)

    def right(t):
        high, low = parts(t)
        return np.block([[high, low], [high, np.zeros_like(low)]])

    def left(t):
        high, low = parts(t)
        return np.block([[high, high], [low, np.zeros_like(low)]])

    return [jnp.asarray(t) for t in (right(b), right(b.T), left(b), left(b.T))]


def per_device(resident, blocks, occupation):
    vmem = pl.BlockSpec(memory_space=pltpu.VMEM)
    hbm = pl.BlockSpec(memory_space=pl.ANY)
    full = pltpu.VMEM((GRID * GRID, GRID), jnp.float32)
    out = pl.pallas_call(
        kernel,
        out_shape=jax.ShapeDtypeStruct((2, ROWS, GRID), jnp.float32),
        in_specs=[hbm, hbm, pl.BlockSpec(memory_space=pltpu.SMEM)] + [vmem] * 4,
        out_specs=vmem,
        scratch_shapes=[
            full,
            full,
            full,
            pltpu.VMEM((GRID * PITCH, GRID), jnp.float32),
            pltpu.VMEM((2, 4, 2, ROWS, GRID), jnp.float32),
            pltpu.VMEM((2, 4, 2, HALF, GRID), jnp.float32),
            pltpu.VMEM((2, 2, ROWS, GRID), jnp.float32),
            pltpu.VMEM((2, 2, HALF, GRID), jnp.float32),
            pltpu.SemaphoreType.DMA((MESSAGES,)),
            pltpu.SemaphoreType.DMA((MESSAGES,)),
            pltpu.SemaphoreType.DMA((2,)),
        ],
        compiler_params=pltpu.CompilerParams(
            collective_id=0, has_side_effects=True, vmem_limit_bytes=56 * 2**20
        ),
        cost_estimate=pl.CostEstimate(flops=13 * 10**9, bytes_accessed=10**7, transcendentals=0),
        name="exchange",
    )(
        resident.reshape(2, ROWS, GRID),
        blocks.reshape(4, ROWS, GRID),
        occupation,
        *tables(),
    )
    return out.reshape(2, PLANES, GRID, GRID)


def solution(mesh):
    placed = (P("band", "slab", None, None), P("band", "slab", None, None), P())
    return jax.shard_map(
        per_device,
        mesh=mesh,
        in_specs=placed,
        out_specs=P("band", "slab", None, None),
        check_vma=False,
    )
```

```python
import math

import jax
import ml_dtypes
import numpy as np
import jax.numpy as jnp
from jax import lax
from jax.experimental import pallas as pl
from jax.experimental.pallas import tpu as pltpu
from jax.sharding import PartitionSpec as P

MESH = pl.DeviceIdType.MESH
PLANES = 4
GRID = 128
ROWS = PLANES * GRID
HALF = ROWS // 2
KAPPA_SQ = 0.01
STEPS = ('s0', 'row', 'c0', 's1', 'far', 'c1', 's2', 'c2', 'own', 'early', 'last')
PITCH = GRID + 8
DEEP = 16


class Place:
    def __init__(self):
        self.band = lax.axis_index("band")
        slab = lax.axis_index("slab")
        self.core = self.band % 2
        self.half = slab // 16
        self.z = (slab // 4) % 4
        self.y = slab % 4
        self.x = self.half * 2 + self.band // 2
        self.stays = jnp.logical_and(self.band == 0, self.z == 0)

    def device(self, dx=0, dy=0, dz=0, flip=False):
        x, y, z = (self.x + dx) % 4, (self.y + dy) % 4, (self.z + dz) % 4
        core = 1 - self.core if flip else self.core
        return ((x % 2) * 2 + core, (x // 2) * 16 + z * 4 + y)

    def piece(self, half, dy=0, dz=0):
        return half * 16 + ((self.z + dz) % 4) * 4 + (self.y + dy) % 4


class Mail:
    def __init__(self, send_sem, recv_sem):
        self.send_sem, self.recv_sem = send_sem, recv_sem
        self.count = 0
        self.sent = []

    def send(self, src, dst, device):
        number = self.count
        self.count += 1
        copy = pltpu.make_async_remote_copy(
            src_ref=src,
            dst_ref=dst,
            send_sem=self.send_sem.at[number],
            recv_sem=self.recv_sem.at[number],
            device_id=device,
            device_id_type=MESH,
        )
        copy.start()
        self.sent.append(copy)
        return number

    def arrive(self, number, dst, device):
        pltpu.make_async_remote_copy(
            src_ref=dst,
            dst_ref=dst,
            send_sem=self.send_sem.at[number],
            recv_sem=self.recv_sem.at[number],
            device_id=device,
            device_id_type=MESH,
        ).wait_recv()

    def finish(self):
        for copy in self.sent:
            copy.wait_send()


def planes(ref, piece, part=None):
    if part is None:
        return ref.at[pl.ds(piece * ROWS, ROWS)]
    return ref.at[pl.ds(piece * ROWS + part * HALF, HALF)]


def greet(me):
    barrier = pltpu.get_barrier_semaphore()
    near = [me.device(dx=1), me.device(dx=3), me.device(dy=1), me.device(dy=3),
            me.device(dz=1), me.device(dz=3), me.device(dx=2), me.device(flip=True)]
    for other in near:
        pl.semaphore_signal(barrier, inc=1, device_id=other, device_id_type=MESH)
    for k in range(1, 4):
        for other in (align_to(me, k), align_from(me, k)):
            pl.semaphore_signal(barrier, inc=1, device_id=other, device_id_type=MESH)

    @pl.when(jnp.logical_not(me.stays))
    def _():
        for other in (align_to(me, 0), align_from(me, 0)):
            pl.semaphore_signal(barrier, inc=1, device_id=other, device_id_type=MESH)
        pl.semaphore_wait(barrier, len(near) + 8)

    @pl.when(me.stays)
    def _():
        pl.semaphore_wait(barrier, len(near) + 6)


def align_to(me, step):
    band = ((me.band + me.z) % 2) * 2 + me.z // 2
    return (band, me.half * 16 + me.band * 4 + (me.y + step) % 4)


def align_z(me, x, core):
    return core * 2 + (x + me.z) % 2


def align_from(me, step):
    return (me.z, me.half * 16 + align_z(me, me.x, me.core) * 4 + (me.y - step) % 4)


class Tree:
    def __init__(self, me, mail, full, half, first):
        self.me, self.mail, self.full, self.half = me, mail, full, half
        self.first = first
        self.box = {}

    def off(self, f, s):
        return dict(dy=f % 4, dz=s % 4) if self.first == "y" else dict(dy=s % 4, dz=f % 4)

    def ref(self, f, s, part=None):
        return planes(self.full, self.me.piece(self.half, **self.off(f, s)), part)

    def push(self, key, src, f, s, df, ds, part=None):
        dst = self.ref(f, s, part)
        self.box[key] = self.mail.send(dst if src is None else src, dst, self.me.device(**self.off(df, ds)))

    def take(self, key, f, s, part=None):
        self.mail.arrive(self.box[key], self.ref(f, s, part), self.me.device(**self.off(0, 0)))

    def start(self, src):
        for d in (1, -1):
            self.push(("f", d), src, 0, 0, d, 0)
        for d in (1, -1):
            self.push(("s", 0, d), src, 0, 0, 0, d)

    def row(self):
        for d in (1, -1):
            self.take(("f", d), -d, 0)
            part = 0 if d == 1 else 1
            self.push(("f2", d), None, -d, 0, d, 0, part)
            for e in (1, -1):
                self.push(("s", -d, e), None, -d, 0, 0, e)

    def column(self, f):
        for e in (1, -1):
            self.take(("s", f, e), f, -e)
            part = 0 if e == 1 else 1
            self.push(("s2", f, e), None, f, -e, 0, e, part)

    def far(self):
        for d in (1, -1):
            self.take(("f2", d), 2, 0, 0 if d == 1 else 1)
        for e in (1, -1):
            self.push(("s", 2, e), None, 2, 0, 0, e)

    def last(self, f):
        for e in (1, -1):
            self.take(("s2", f, e), f, 2, 0 if e == 1 else 1)


def split(v):
    high = v.astype(jnp.bfloat16)
    return high, (v - high.astype(jnp.float32)).astype(jnp.bfloat16)


def times(v, table):
    r = jnp.dot(jnp.concatenate(split(v), axis=1), table, preferred_element_type=jnp.float32)
    return r[:, :GRID] + r[:, GRID:]


def under(table, va, vb):
    (ha, la), (hb, lb) = split(va), split(vb)
    values = jnp.concatenate([jnp.concatenate([ha, hb], axis=1), jnp.concatenate([la, lb], axis=1)], axis=0)
    r = jnp.dot(table, values, preferred_element_type=jnp.float32)
    r = r[:GRID] + r[GRID:]
    return r[:, :GRID], r[:, GRID:]


def gather(me, mail, res_ref, blk_ref, rfull, sfull, local_sem, fetches, forward):
    send_sem, recv_sem = mail.send_sem, mail.recv_sem
    h = me.half
    mine = me.piece(h)

    def spiece(dx, flip, t):
        x = (me.x + dx) % 4
        core = 1 - me.core if flip else me.core
        return (x // 2) * 16 + align_z(me, x, core) * 4 + (me.y + t) % 4

    order = (0, 1, 3, 2)
    align_no = {}
    for t in order:
        number = mail.count
        mail.count += 1
        align_no[t] = number
        src = blk_ref.at[(me.y + t) % 4]
        dst = planes(sfull, mine)

        def remote(src=src, dst=dst, t=t, number=number):
            return pltpu.make_async_remote_copy(
                src_ref=src, dst_ref=dst, send_sem=send_sem.at[number], recv_sem=recv_sem.at[number],
                device_id=align_to(me, t), device_id_type=MESH)
        if t:
            copy = remote()
            copy.start()
            mail.sent.append(copy)
        else:
            @pl.when(jnp.logical_not(me.stays))
            def _():
                remote().start()

            @pl.when(me.stays)
            def _():
                pltpu.make_async_copy(src, dst, local_sem.at[1]).start()
            zero = (remote, src, dst)
    swap = mail.send(res_ref.at[1 - h], planes(rfull, mine), me.device(dx=2))
    tree_a = Tree(me, mail, rfull, h, "y")
    tree_b = Tree(me, mail, rfull, 1 - h, "z")
    tree_a.start(res_ref.at[h])
    own = pltpu.make_async_copy(res_ref.at[h], planes(rfull, mine), local_sem.at[0])
    own.start()
    mail.arrive(swap, planes(rfull, me.piece(1 - h)), me.device(dx=2))
    tree_b.start(None)

    xs = {}
    backs = [-t % 4 for t in order]
    trees = (tree_a, tree_b)

    def collected():
        for t in order:
            back = -t % 4
            dst = planes(sfull, spiece(0, False, back))
            if t:
                mail.arrive(align_no[t], dst, align_from(me, t))
            else:
                @pl.when(jnp.logical_not(me.stays))
                def _():
                    zero[0]().wait_recv()

                @pl.when(me.stays)
                def _():
                    pltpu.make_async_copy(zero[1], zero[2], local_sem.at[1]).wait()
            for d in (1, -1):
                xs[("x", d, back)] = mail.send(dst, dst, me.device(dx=d))
            xs[("c", 0, back)] = mail.send(dst, dst, me.device(flip=True))

    def beside():
        for t in backs:
            for d in (1, -1):
                ref = planes(sfull, spiece(-d, False, t))
                mail.arrive(xs[("x", d, t)], ref, me.device(dx=-d))
                part = 0 if d == 1 else 1
                ref2 = planes(sfull, spiece(-d, False, t), part)
                xs[("x2", d, t)] = mail.send(ref2, ref2, me.device(dx=d))
                xs[("c", -d, t)] = mail.send(ref, ref, me.device(flip=True))

    def across():
        for t in backs:
            for d in (1, -1):
                ref2 = planes(sfull, spiece(2, False, t), 0 if d == 1 else 1)
                mail.arrive(xs[("x2", d, t)], ref2, me.device(dx=-d))
            ref = planes(sfull, spiece(2, False, t))
            xs[("c", 2, t)] = mail.send(ref, ref, me.device(flip=True))

    def column(*offsets):
        for f in offsets:
            for tree in trees:
                tree.column(f)

    def ready(late):
        for dx in (0, -1, 1, 2):
            x = (me.x + dx) % 4
            same = x // 2 == h
            close = align_z(me, x, me.core) != (me.z + 2) % 4
            whole = jnp.logical_and(same, jnp.logical_not(close) if late else close)

            @pl.when(whole)
            def _():
                forward([spiece(dx, False, t) for t in range(4)])

            @pl.when(jnp.logical_not(same))
            def _():
                forward([spiece(dx, False, t) for t in ((2,) if late else (0, 1, 3))])

    steps = {
        "own": lambda: [copy.wait() for copy in (own, *fetches)],
        "row": lambda: [tree.row() for tree in trees],
        "far": lambda: [tree.far() for tree in trees],
        "c0": lambda: column(0),
        "c1": lambda: column(-1, 1),
        "c2": lambda: column(2),
        "last": lambda: [tree.last(f) for f in (0, -1, 1, 2) for tree in trees],
        "early": lambda: ready(False),
        "s0": collected,
        "s1": beside,
        "s2": across,
    }
    for step in STEPS:
        steps[step]()
    ready(True)
    for dx in (0, -1, 1, 2):
        for t in backs:
            mail.arrive(xs[("c", dx, t)], planes(sfull, spiece(dx, True, t)), me.device(flip=True))
        forward([spiece(dx, True, t) for t in backs])

    def finish():
        @pl.when(jnp.logical_not(me.stays))
        def _():
            zero[0]().wait_send()

    return finish


class Sum:
    def __init__(self, me, mail, term, near_s, far_s, near_f, far_f, half, first):
        self.me, self.mail, self.term = me, mail, term
        self.near_s, self.far_s, self.near_f, self.far_f = near_s, far_s, near_f, far_f
        self.half, self.first = half, first
        self.box = {}

    def off(self, f, s):
        return dict(dy=f % 4, dz=s % 4) if self.first == "y" else dict(dy=s % 4, dz=f % 4)

    def ref(self, f, s, part=None):
        return planes(self.term, self.me.piece(self.half, **self.off(f, s)), part)

    def slots(self, d, f=None):
        n = 0 if d == 1 else 1
        if f is None:
            return self.far_f.at[n], self.near_f.at[n]
        return self.far_s.at[f % 4, n], self.near_s.at[f % 4, n]

    def post(self, key, src, dst, df, ds):
        self.box[key] = self.mail.send(src, dst, self.me.device(**self.off(df, ds)))

    def add(self, key, into, slot):
        self.mail.arrive(self.box[key], slot, self.me.device())
        into[...] += slot[...]

    def far_column(self, f):
        for e in (1, -1):
            self.post(("a", f, e), self.ref(f, 2, 0 if e == 1 else 1), self.slots(e, f)[0], 0, e)

    def near_column(self, f):
        for e in (1, -1):
            self.add(("a", f, e), self.ref(f, e, 0 if e == 1 else 1), self.slots(e, f)[0])
            self.post(("b", f, e), self.ref(f, e), self.slots(e, f)[1], 0, e)

    def own_column(self, f):
        for e in (1, -1):
            self.add(("b", f, e), self.ref(f, 0), self.slots(e, f)[1])

    def far_row(self):
        for d in (1, -1):
            self.post(("c", d), self.ref(2, 0, 0 if d == 1 else 1), self.slots(d)[0], d, 0)

    def near_row(self, d):
        self.add(("c", d), self.ref(d, 0, 0 if d == 1 else 1), self.slots(d)[0])
        self.post(("d", d), self.ref(d, 0), self.slots(d)[1], d, 0)

    def own_row(self):
        for d in (1, -1):
            self.add(("d", d), self.ref(0, 0), self.slots(d)[1])


def kernel(res_ref, blk_ref, occ_ref, tables_ref, out_ref, right_ref, right_t_ref, left_ref, left_t_ref,
           rfull, sfull, term, work, near_s, far_s, near_f, far_f, send_sem, recv_sem, local_sem):
    me = Place()
    fetches = [
        pltpu.make_async_copy(tables_ref.at[n], ref, local_sem.at[2 + n])
        for n, ref in enumerate((right_ref, right_t_ref, left_ref, left_t_ref))
    ]
    for fetch in fetches:
        fetch.start()
    greet(me)
    mail = Mail(send_sem, recv_sem)
    h = me.half
    weight = -occ_ref[me.z * 4 + me.y]

    def units(pieces, n):
        return [pl.multiple_of(piece * ROWS + n * 2 * GRID, 2 * GRID) for piece in pieces]

    def pitched(start):
        first = pl.multiple_of(start // GRID * PITCH, 8)
        return pl.ds(first, GRID), pl.ds(pl.multiple_of(first + PITCH, 8), GRID)

    def forward(pieces):
        @pl.loop(0, PLANES // 2)
        def _(n):
            for start in units(pieces, n):
                rows = pl.ds(start, 2 * GRID)
                v = times(rfull[rows, :] * sfull[rows, :], right_ref[...])
                va, vb = under(left_t_ref[...], v[:GRID], v[GRID:])
                one, two = pitched(start)
                work[one, :] = va
                work[two, :] = vb

    def backward(pieces):
        @pl.loop(0, PLANES // 2)
        def _(n):
            starts = units(pieces, n)
            held = [[work[rows, :] for rows in pitched(start)] for start in starts]
            results = []
            for start, values in zip(starts, held):
                va, vb = under(left_ref[...], *values)
                v = times(jnp.concatenate([va, vb], axis=0), right_t_ref[...])
                results.append(v * (sfull[pl.ds(start, 2 * GRID), :] * weight))
            for start, v in zip(starts, results):
                term[pl.ds(start, 2 * GRID), :] = v

    finish = gather(me, mail, res_ref, blk_ref, rfull, sfull, local_sem, fetches, forward)

    def wave_sq(index):
        signed = jnp.minimum(index, GRID - index).astype(jnp.float32) * (2.0 * math.pi / GRID)
        return signed * signed

    shape = (GRID, GRID)
    base = wave_sq(lax.broadcasted_iota(jnp.int32, shape, 0)) + wave_sq(lax.broadcasted_iota(jnp.int32, shape, 1)) + KAPPA_SQ

    @pl.loop(0, GRID // (2 * DEEP))
    def _(n):
        indices = [(n * 2 * DEEP + 2 * k, n * 2 * DEEP + 2 * k + 1) for k in range(DEEP)]
        held = [[work[pl.ds(i, GRID, stride=PITCH), :] for i in pair] for pair in indices]
        results = []
        for pair, values in zip(indices, held):
            values = under(left_t_ref[...], *values)
            values = [v * (4.0 * math.pi / (base + wave_sq(i))) for i, v in zip(pair, values)]
            results.append(under(left_ref[...], *values))
        for pair, values in zip(indices, results):
            for i, v in zip(pair, values):
                work[pl.ds(i, GRID, stride=PITCH), :] = v

    sums = [
        Sum(me, mail, term, near_s.at[n], far_s.at[n], near_f.at[n], far_f.at[n], half, first)
        for n, (half, first) in enumerate(((1 - h, "z"), (h, "y")))
    ]
    def pieces(s, f, off):
        return [me.piece(s.half, **s.off(f, off))]

    def far(f):
        backward([p for s in sums for p in pieces(s, f, 2)])
        for s in sums:
            s.far_column(f)

    def near(f):
        backward([p for s in sums for e in (1, -1) for p in pieces(s, f, e)])
        for s in sums:
            s.near_column(f)

    def own(f):
        backward([p for s in sums for p in pieces(s, f, 0)])
        for s in sums:
            s.own_column(f)
        for s in sums:
            if f == 2:
                s.far_row()
            elif f:
                s.near_row(f)

    for step, f in (
        (far, 2), (far, 1), (far, -1), (near, 2), (far, 0), (near, 1), (near, -1), (own, 2),
        (near, 0), (own, 1), (own, -1), (own, 0),
    ):
        step(f)
    sums[0].own_row()
    swap = mail.send(planes(term, me.piece(1 - h)), out_ref.at[h], me.device(dx=2))
    sums[1].own_row()
    mail.arrive(swap, out_ref.at[1 - h], me.device(dx=2))
    mail.finish()
    out_ref[h] = planes(term, me.piece(h))[...]
    finish()


MESSAGES = 77 + 41


def basis():
    points = np.arange(GRID)
    freqs = np.minimum(points, GRID - points)
    angles = 2.0 * np.pi * ((points[:, None] * freqs[None, :]) % GRID) / GRID
    table = np.where(points[None, :] > GRID // 2, np.sin(angles), np.cos(angles)) * np.sqrt(2.0 / GRID)
    table[:, 0] /= np.sqrt(2.0)
    table[:, GRID // 2] /= np.sqrt(2.0)
    return table


def tables():
    b = basis()

    def parts(t):
        high = t.astype(ml_dtypes.bfloat16)
        return high, (t - high.astype(np.float64)).astype(ml_dtypes.bfloat16)

    def right(t):
        high, low = parts(t)
        return np.block([[high, low], [high, np.zeros_like(low)]])

    def left(t):
        high, low = parts(t)
        return np.block([[high, high], [low, np.zeros_like(low)]])

    return jnp.asarray(np.stack([right(b), right(b.T), left(b), left(b.T)]))


def per_device(resident, blocks, occupation):
    vmem = pl.BlockSpec(memory_space=pltpu.VMEM)
    hbm = pl.BlockSpec(memory_space=pl.ANY)
    full = pltpu.VMEM((GRID * GRID, GRID), jnp.float32)
    out = pl.pallas_call(
        kernel,
        out_shape=jax.ShapeDtypeStruct((2, ROWS, GRID), jnp.float32),
        in_specs=[hbm, hbm, pl.BlockSpec(memory_space=pltpu.SMEM), hbm],
        out_specs=vmem,
        scratch_shapes=[
            *[pltpu.VMEM((2 * GRID, 2 * GRID), jnp.bfloat16)] * 4,
            full,
            full,
            full,
            pltpu.VMEM((GRID * PITCH, GRID), jnp.float32),
            pltpu.VMEM((2, 4, 2, ROWS, GRID), jnp.float32),
            pltpu.VMEM((2, 4, 2, HALF, GRID), jnp.float32),
            pltpu.VMEM((2, 2, ROWS, GRID), jnp.float32),
            pltpu.VMEM((2, 2, HALF, GRID), jnp.float32),
            pltpu.SemaphoreType.DMA((MESSAGES,)),
            pltpu.SemaphoreType.DMA((MESSAGES,)),
            pltpu.SemaphoreType.DMA((6,)),
        ],
        compiler_params=pltpu.CompilerParams(
            collective_id=0, has_side_effects=True, vmem_limit_bytes=56 * 2**20
        ),
        cost_estimate=pl.CostEstimate(flops=13 * 10**9, bytes_accessed=10**7, transcendentals=0),
        name="exchange",
    )(
        resident.reshape(2, ROWS, GRID),
        blocks.reshape(4, ROWS, GRID),
        occupation,
        tables(),
    )
    return out.reshape(2, PLANES, GRID, GRID)


def solution(mesh):
    placed = (P("band", "slab", None, None), P("band", "slab", None, None), P())
    return jax.shard_map(
        per_device,
        mesh=mesh,
        in_specs=placed,
        out_specs=P("band", "slab", None, None),
        check_vma=False,
    )
```

```python
import math

import jax
import ml_dtypes
import numpy as np
import jax.numpy as jnp
from jax import lax
from jax.experimental import pallas as pl
from jax.experimental.pallas import tpu as pltpu
from jax.sharding import PartitionSpec as P

MESH = pl.DeviceIdType.MESH
PLANES = 4
GRID = 128
ROWS = PLANES * GRID
HALF = ROWS // 2
KAPPA_SQ = 0.01
STEPS = ('s0', 'row', 'c0', 's1', 'far', 'c1', 's2', 'c2', 'own', 'early', 'last')
PITCH = GRID + 8
DEEP = 16


class Place:
    def __init__(self):
        self.band = lax.axis_index("band")
        slab = lax.axis_index("slab")
        self.core = self.band % 2
        self.half = slab // 16
        self.z = (slab // 4) % 4
        self.y = slab % 4
        self.x = self.half * 2 + self.band // 2
        self.stays = jnp.logical_and(self.band == 0, self.z == 0)

    def device(self, dx=0, dy=0, dz=0, flip=False):
        x, y, z = (self.x + dx) % 4, (self.y + dy) % 4, (self.z + dz) % 4
        core = 1 - self.core if flip else self.core
        return ((x % 2) * 2 + core, (x // 2) * 16 + z * 4 + y)

    def piece(self, half, dy=0, dz=0):
        return half * 16 + ((self.z + dz) % 4) * 4 + (self.y + dy) % 4


class Mail:
    def __init__(self, send_sem, recv_sem):
        self.send_sem, self.recv_sem = send_sem, recv_sem
        self.count = 0
        self.sent = []

    def send(self, src, dst, device):
        number = self.count
        self.count += 1
        copy = pltpu.make_async_remote_copy(
            src_ref=src,
            dst_ref=dst,
            send_sem=self.send_sem.at[number],
            recv_sem=self.recv_sem.at[number],
            device_id=device,
            device_id_type=MESH,
        )
        copy.start()
        self.sent.append(copy)
        return number

    def arrive(self, number, dst, device):
        pltpu.make_async_remote_copy(
            src_ref=dst,
            dst_ref=dst,
            send_sem=self.send_sem.at[number],
            recv_sem=self.recv_sem.at[number],
            device_id=device,
            device_id_type=MESH,
        ).wait_recv()

    def finish(self):
        for copy in self.sent:
            copy.wait_send()


def planes(ref, piece, part=None):
    if part is None:
        return ref.at[pl.ds(piece * ROWS, ROWS)]
    return ref.at[pl.ds(piece * ROWS + part * HALF, HALF)]


def greet(me):
    barrier = pltpu.get_barrier_semaphore()
    near = [me.device(dx=1), me.device(dx=3), me.device(dy=1), me.device(dy=3),
            me.device(dz=1), me.device(dz=3), me.device(dx=2), me.device(flip=True)]
    for other in near:
        pl.semaphore_signal(barrier, inc=1, device_id=other, device_id_type=MESH)
    for k in range(1, 4):
        for other in (align_to(me, k), align_from(me, k)):
            pl.semaphore_signal(barrier, inc=1, device_id=other, device_id_type=MESH)

    @pl.when(jnp.logical_not(me.stays))
    def _():
        for other in (align_to(me, 0), align_from(me, 0)):
            pl.semaphore_signal(barrier, inc=1, device_id=other, device_id_type=MESH)
        pl.semaphore_wait(barrier, len(near) + 8)

    @pl.when(me.stays)
    def _():
        pl.semaphore_wait(barrier, len(near) + 6)


def align_to(me, step):
    band = ((me.band + me.z) % 2) * 2 + me.z // 2
    return (band, me.half * 16 + me.band * 4 + (me.y + step) % 4)


def align_z(me, x, core):
    return core * 2 + (x + me.z) % 2


def align_from(me, step):
    return (me.z, me.half * 16 + align_z(me, me.x, me.core) * 4 + (me.y - step) % 4)


class Tree:
    def __init__(self, me, mail, full, half, first):
        self.me, self.mail, self.full, self.half = me, mail, full, half
        self.first = first
        self.box = {}

    def off(self, f, s):
        return dict(dy=f % 4, dz=s % 4) if self.first == "y" else dict(dy=s % 4, dz=f % 4)

    def ref(self, f, s, part=None):
        return planes(self.full, self.me.piece(self.half, **self.off(f, s)), part)

    def push(self, key, src, f, s, df, ds, part=None):
        dst = self.ref(f, s, part)
        self.box[key] = self.mail.send(dst if src is None else src, dst, self.me.device(**self.off(df, ds)))

    def take(self, key, f, s, part=None):
        self.mail.arrive(self.box[key], self.ref(f, s, part), self.me.device(**self.off(0, 0)))

    def start(self, src):
        for d in (1, -1):
            self.push(("f", d), src, 0, 0, d, 0)
        for d in (1, -1):
            self.push(("s", 0, d), src, 0, 0, 0, d)

    def row(self):
        for d in (1, -1):
            self.take(("f", d), -d, 0)
            part = 0 if d == 1 else 1
            self.push(("f2", d), None, -d, 0, d, 0, part)
            for e in (1, -1):
                self.push(("s", -d, e), None, -d, 0, 0, e)

    def column(self, f):
        for e in (1, -1):
            self.take(("s", f, e), f, -e)
            part = 0 if e == 1 else 1
            self.push(("s2", f, e), None, f, -e, 0, e, part)

    def far(self):
        for d in (1, -1):
            self.take(("f2", d), 2, 0, 0 if d == 1 else 1)
        for e in (1, -1):
            self.push(("s", 2, e), None, 2, 0, 0, e)

    def last(self, f):
        for e in (1, -1):
            self.take(("s2", f, e), f, 2, 0 if e == 1 else 1)


def split(v):
    high = v.astype(jnp.bfloat16)
    return high, (v - high.astype(jnp.float32)).astype(jnp.bfloat16)


def times(v, table):
    r = jnp.dot(jnp.concatenate(split(v), axis=1), table, preferred_element_type=jnp.float32)
    return r[:, :GRID] + r[:, GRID:]


def under(table, va, vb):
    (ha, la), (hb, lb) = split(va), split(vb)
    values = jnp.concatenate([jnp.concatenate([ha, hb], axis=1), jnp.concatenate([la, lb], axis=1)], axis=0)
    r = jnp.dot(table, values, preferred_element_type=jnp.float32)
    r = r[:GRID] + r[GRID:]
    return r[:, :GRID], r[:, GRID:]


def gather(me, mail, res_ref, blk_ref, rfull, sfull, local_sem, fetches, forward):
    send_sem, recv_sem = mail.send_sem, mail.recv_sem
    h = me.half
    mine = me.piece(h)

    def spiece(dx, flip, t):
        x = (me.x + dx) % 4
        core = 1 - me.core if flip else me.core
        return (x // 2) * 16 + align_z(me, x, core) * 4 + (me.y + t) % 4

    swap = mail.send(res_ref.at[1 - h], planes(rfull, mine), me.device(dx=2))
    order = (0, 1, 3, 2)
    align_no = {}
    for t in order:
        number = mail.count
        mail.count += 1
        align_no[t] = number
        src = blk_ref.at[(me.y + t) % 4]
        dst = planes(sfull, mine)

        def remote(src=src, dst=dst, t=t, number=number):
            return pltpu.make_async_remote_copy(
                src_ref=src, dst_ref=dst, send_sem=send_sem.at[number], recv_sem=recv_sem.at[number],
                device_id=align_to(me, t), device_id_type=MESH)
        if t:
            copy = remote()
            copy.start()
            mail.sent.append(copy)
        else:
            @pl.when(jnp.logical_not(me.stays))
            def _():
                remote().start()

            @pl.when(me.stays)
            def _():
                pltpu.make_async_copy(src, dst, local_sem.at[1]).start()
            zero = (remote, src, dst)
    tree_a = Tree(me, mail, rfull, h, "y")
    tree_b = Tree(me, mail, rfull, 1 - h, "z")
    tree_a.start(res_ref.at[h])
    own = pltpu.make_async_copy(res_ref.at[h], planes(rfull, mine), local_sem.at[0])
    own.start()
    mail.arrive(swap, planes(rfull, me.piece(1 - h)), me.device(dx=2))
    tree_b.start(None)

    xs = {}
    backs = [-t % 4 for t in order]
    trees = (tree_a, tree_b)

    def collected():
        for t in order:
            back = -t % 4
            dst = planes(sfull, spiece(0, False, back))
            if t:
                mail.arrive(align_no[t], dst, align_from(me, t))
            else:
                @pl.when(jnp.logical_not(me.stays))
                def _():
                    zero[0]().wait_recv()

                @pl.when(me.stays)
                def _():
                    pltpu.make_async_copy(zero[1], zero[2], local_sem.at[1]).wait()
            for d in (1, -1):
                xs[("x", d, back)] = mail.send(dst, dst, me.device(dx=d))
            xs[("c", 0, back)] = mail.send(dst, dst, me.device(flip=True))

    def beside():
        for t in backs:
            for d in (1, -1):
                ref = planes(sfull, spiece(-d, False, t))
                mail.arrive(xs[("x", d, t)], ref, me.device(dx=-d))
                part = 0 if d == 1 else 1
                ref2 = planes(sfull, spiece(-d, False, t), part)
                xs[("x2", d, t)] = mail.send(ref2, ref2, me.device(dx=d))
                xs[("c", -d, t)] = mail.send(ref, ref, me.device(flip=True))

    def across():
        for t in backs:
            for d in (1, -1):
                ref2 = planes(sfull, spiece(2, False, t), 0 if d == 1 else 1)
                mail.arrive(xs[("x2", d, t)], ref2, me.device(dx=-d))
            ref = planes(sfull, spiece(2, False, t))
            xs[("c", 2, t)] = mail.send(ref, ref, me.device(flip=True))

    def column(*offsets):
        for f in offsets:
            for tree in trees:
                tree.column(f)

    def ready(late):
        for dx in (0, -1, 1, 2):
            x = (me.x + dx) % 4
            same = x // 2 == h
            close = align_z(me, x, me.core) != (me.z + 2) % 4
            whole = jnp.logical_and(same, jnp.logical_not(close) if late else close)

            @pl.when(whole)
            def _():
                forward([spiece(dx, False, t) for t in range(4)])

            @pl.when(jnp.logical_not(same))
            def _():
                forward([spiece(dx, False, t) for t in ((2,) if late else (0, 1, 3))])

    steps = {
        "own": lambda: [copy.wait() for copy in (own, *fetches)],
        "row": lambda: [tree.row() for tree in trees],
        "far": lambda: [tree.far() for tree in trees],
        "c0": lambda: column(0),
        "c1": lambda: column(-1, 1),
        "c2": lambda: column(2),
        "last": lambda: [tree.last(f) for f in (0, -1, 1, 2) for tree in trees],
        "early": lambda: ready(False),
        "s0": collected,
        "s1": beside,
        "s2": across,
    }
    for step in STEPS:
        steps[step]()
    ready(True)
    for dx in (0, -1, 1, 2):
        for t in backs:
            mail.arrive(xs[("c", dx, t)], planes(sfull, spiece(dx, True, t)), me.device(flip=True))
        forward([spiece(dx, True, t) for t in backs])

    def finish():
        @pl.when(jnp.logical_not(me.stays))
        def _():
            zero[0]().wait_send()

    return finish


class Sum:
    def __init__(self, me, mail, term, near_s, far_s, near_f, far_f, half, first):
        self.me, self.mail, self.term = me, mail, term
        self.near_s, self.far_s, self.near_f, self.far_f = near_s, far_s, near_f, far_f
        self.half, self.first = half, first
        self.box = {}

    def off(self, f, s):
        return dict(dy=f % 4, dz=s % 4) if self.first == "y" else dict(dy=s % 4, dz=f % 4)

    def ref(self, f, s, part=None):
        return planes(self.term, self.me.piece(self.half, **self.off(f, s)), part)

    def slots(self, d, f=None):
        n = 0 if d == 1 else 1
        if f is None:
            return self.far_f.at[n], self.near_f.at[n]
        return self.far_s.at[f % 4, n], self.near_s.at[f % 4, n]

    def post(self, key, src, dst, df, ds):
        self.box[key] = self.mail.send(src, dst, self.me.device(**self.off(df, ds)))

    def add(self, key, into, slot):
        self.mail.arrive(self.box[key], slot, self.me.device())
        into[...] += slot[...]

    def far_column(self, f):
        for e in (1, -1):
            self.post(("a", f, e), self.ref(f, 2, 0 if e == 1 else 1), self.slots(e, f)[0], 0, e)

    def near_column(self, f):
        for e in (1, -1):
            self.add(("a", f, e), self.ref(f, e, 0 if e == 1 else 1), self.slots(e, f)[0])
            self.post(("b", f, e), self.ref(f, e), self.slots(e, f)[1], 0, e)

    def own_column(self, f):
        for e in (1, -1):
            self.add(("b", f, e), self.ref(f, 0), self.slots(e, f)[1])

    def far_row(self):
        for d in (1, -1):
            self.post(("c", d), self.ref(2, 0, 0 if d == 1 else 1), self.slots(d)[0], d, 0)

    def near_row(self, d):
        self.add(("c", d), self.ref(d, 0, 0 if d == 1 else 1), self.slots(d)[0])
        self.post(("d", d), self.ref(d, 0), self.slots(d)[1], d, 0)

    def own_row(self):
        for d in (1, -1):
            self.add(("d", d), self.ref(0, 0), self.slots(d)[1])


def kernel(res_ref, blk_ref, occ_ref, tables_ref, out_ref, right_ref, right_t_ref, left_ref, left_t_ref,
           rfull, sfull, term, work, near_s, far_s, near_f, far_f, send_sem, recv_sem, local_sem):
    me = Place()
    fetches = [
        pltpu.make_async_copy(tables_ref.at[n], ref, local_sem.at[2 + n])
        for n, ref in enumerate((right_ref, right_t_ref, left_ref, left_t_ref))
    ]
    for fetch in fetches:
        fetch.start()
    greet(me)
    mail = Mail(send_sem, recv_sem)
    h = me.half
    weight = -occ_ref[me.z * 4 + me.y]

    def units(pieces, n):
        return [pl.multiple_of(piece * ROWS + n * 2 * GRID, 2 * GRID) for piece in pieces]

    def pitched(start):
        first = pl.multiple_of(start // GRID * PITCH, 8)
        return pl.ds(first, GRID), pl.ds(pl.multiple_of(first + PITCH, 8), GRID)

    def forward(pieces):
        @pl.loop(0, PLANES // 2)
        def _(n):
            for start in units(pieces, n):
                rows = pl.ds(start, 2 * GRID)
                v = times(rfull[rows, :] * sfull[rows, :], right_ref[...])
                va, vb = under(left_t_ref[...], v[:GRID], v[GRID:])
                one, two = pitched(start)
                work[one, :] = va
                work[two, :] = vb

    def backward(pieces):
        @pl.loop(0, PLANES // 2)
        def _(n):
            starts = units(pieces, n)
            held = [[work[rows, :] for rows in pitched(start)] for start in starts]
            results = []
            for start, values in zip(starts, held):
                va, vb = under(left_ref[...], *values)
                v = times(jnp.concatenate([va, vb], axis=0), right_t_ref[...])
                results.append(v * (sfull[pl.ds(start, 2 * GRID), :] * weight))
            for start, v in zip(starts, results):
                term[pl.ds(start, 2 * GRID), :] = v

    finish = gather(me, mail, res_ref, blk_ref, rfull, sfull, local_sem, fetches, forward)

    def wave_sq(index):
        signed = jnp.minimum(index, GRID - index).astype(jnp.float32) * (2.0 * math.pi / GRID)
        return signed * signed

    shape = (GRID, GRID)
    base = wave_sq(lax.broadcasted_iota(jnp.int32, shape, 0)) + wave_sq(lax.broadcasted_iota(jnp.int32, shape, 1)) + KAPPA_SQ

    @pl.loop(0, GRID // (2 * DEEP))
    def _(n):
        indices = [(n * 2 * DEEP + 2 * k, n * 2 * DEEP + 2 * k + 1) for k in range(DEEP)]
        held = [[work[pl.ds(i, GRID, stride=PITCH), :] for i in pair] for pair in indices]
        results = []
        for pair, values in zip(indices, held):
            values = under(left_t_ref[...], *values)
            values = [v * (4.0 * math.pi / (base + wave_sq(i))) for i, v in zip(pair, values)]
            results.append(under(left_ref[...], *values))
        for pair, values in zip(indices, results):
            for i, v in zip(pair, values):
                work[pl.ds(i, GRID, stride=PITCH), :] = v

    sums = [
        Sum(me, mail, term, near_s.at[n], far_s.at[n], near_f.at[n], far_f.at[n], half, first)
        for n, (half, first) in enumerate(((1 - h, "z"), (h, "y")))
    ]
    def pieces(s, f, off):
        return [me.piece(s.half, **s.off(f, off))]

    def far(f):
        backward([p for s in sums for p in pieces(s, f, 2)])
        for s in sums:
            s.far_column(f)

    def near(f):
        backward([p for s in sums for e in (1, -1) for p in pieces(s, f, e)])
        for s in sums:
            s.near_column(f)

    def own(f):
        backward([p for s in sums for p in pieces(s, f, 0)])
        for s in sums:
            s.own_column(f)
        for s in sums:
            if f == 2:
                s.far_row()
            elif f:
                s.near_row(f)

    for step, f in (
        (far, 2), (far, 1), (far, -1), (near, 2), (far, 0), (near, 1), (near, -1), (own, 2),
        (near, 0), (own, 1), (own, -1), (own, 0),
    ):
        step(f)
    sums[0].own_row()
    swap = mail.send(planes(term, me.piece(1 - h)), out_ref.at[h], me.device(dx=2))
    sums[1].own_row()
    mail.arrive(swap, out_ref.at[1 - h], me.device(dx=2))
    mail.finish()
    out_ref[h] = planes(term, me.piece(h))[...]
    finish()


MESSAGES = 77 + 41


def basis():
    points = np.arange(GRID)
    freqs = np.minimum(points, GRID - points)
    angles = 2.0 * np.pi * ((points[:, None] * freqs[None, :]) % GRID) / GRID
    table = np.where(points[None, :] > GRID // 2, np.sin(angles), np.cos(angles)) * np.sqrt(2.0 / GRID)
    table[:, 0] /= np.sqrt(2.0)
    table[:, GRID // 2] /= np.sqrt(2.0)
    return table


def tables():
    b = basis()

    def parts(t):
        high = t.astype(ml_dtypes.bfloat16)
        return high, (t - high.astype(np.float64)).astype(ml_dtypes.bfloat16)

    def right(t):
        high, low = parts(t)
        return np.block([[high, low], [high, np.zeros_like(low)]])

    def left(t):
        high, low = parts(t)
        return np.block([[high, high], [low, np.zeros_like(low)]])

    return jnp.asarray(np.stack([right(b), right(b.T), left(b), left(b.T)]))


def per_device(resident, blocks, occupation):
    vmem = pl.BlockSpec(memory_space=pltpu.VMEM)
    hbm = pl.BlockSpec(memory_space=pl.ANY)
    full = pltpu.VMEM((GRID * GRID, GRID), jnp.float32)
    out = pl.pallas_call(
        kernel,
        out_shape=jax.ShapeDtypeStruct((2, ROWS, GRID), jnp.float32),
        in_specs=[hbm, hbm, pl.BlockSpec(memory_space=pltpu.SMEM), hbm],
        out_specs=vmem,
        scratch_shapes=[
            *[pltpu.VMEM((2 * GRID, 2 * GRID), jnp.bfloat16)] * 4,
            full,
            full,
            full,
            pltpu.VMEM((GRID * PITCH, GRID), jnp.float32),
            pltpu.VMEM((2, 4, 2, ROWS, GRID), jnp.float32),
            pltpu.VMEM((2, 4, 2, HALF, GRID), jnp.float32),
            pltpu.VMEM((2, 2, ROWS, GRID), jnp.float32),
            pltpu.VMEM((2, 2, HALF, GRID), jnp.float32),
            pltpu.SemaphoreType.DMA((MESSAGES,)),
            pltpu.SemaphoreType.DMA((MESSAGES,)),
            pltpu.SemaphoreType.DMA((6,)),
        ],
        compiler_params=pltpu.CompilerParams(
            collective_id=0, has_side_effects=True, vmem_limit_bytes=56 * 2**20
        ),
        cost_estimate=pl.CostEstimate(flops=13 * 10**9, bytes_accessed=10**7, transcendentals=0),
        name="exchange",
    )(
        resident.reshape(2, ROWS, GRID),
        blocks.reshape(4, ROWS, GRID),
        occupation,
        tables(),
    )
    return out.reshape(2, PLANES, GRID, GRID)


def solution(mesh):
    placed = (P("band", "slab", None, None), P("band", "slab", None, None), P())
    return jax.shard_map(
        per_device,
        mesh=mesh,
        in_specs=placed,
        out_specs=P("band", "slab", None, None),
        check_vma=False,
    )
```

```python
import math

import jax
import ml_dtypes
import numpy as np
import jax.numpy as jnp
from jax import lax
from jax.experimental import pallas as pl
from jax.experimental.pallas import tpu as pltpu
from jax.sharding import PartitionSpec as P

MESH = pl.DeviceIdType.MESH
PLANES = 4
GRID = 128
ROWS = PLANES * GRID
HALF = ROWS // 2
KAPPA_SQ = 0.01
STEPS = ('s0', 'row', 'c0', 's1', 'far', 'c1', 's2', 'c2', 'own', 'early', 'last')
PITCH = GRID + 8
DEEP = 32


class Place:
    def __init__(self):
        self.band = lax.axis_index("band")
        slab = lax.axis_index("slab")
        self.core = self.band % 2
        self.half = slab // 16
        self.z = (slab // 4) % 4
        self.y = slab % 4
        self.x = self.half * 2 + self.band // 2
        self.stays = jnp.logical_and(self.band == 0, self.z == 0)

    def device(self, dx=0, dy=0, dz=0, flip=False):
        x, y, z = (self.x + dx) % 4, (self.y + dy) % 4, (self.z + dz) % 4
        core = 1 - self.core if flip else self.core
        return ((x % 2) * 2 + core, (x // 2) * 16 + z * 4 + y)

    def piece(self, half, dy=0, dz=0):
        return half * 16 + ((self.z + dz) % 4) * 4 + (self.y + dy) % 4


class Mail:
    def __init__(self, send_sem, recv_sem):
        self.send_sem, self.recv_sem = send_sem, recv_sem
        self.count = 0
        self.sent = []

    def send(self, src, dst, device):
        number = self.count
        self.count += 1
        copy = pltpu.make_async_remote_copy(
            src_ref=src,
            dst_ref=dst,
            send_sem=self.send_sem.at[number],
            recv_sem=self.recv_sem.at[number],
            device_id=device,
            device_id_type=MESH,
        )
        copy.start()
        self.sent.append(copy)
        return number

    def arrive(self, number, dst, device):
        pltpu.make_async_remote_copy(
            src_ref=dst,
            dst_ref=dst,
            send_sem=self.send_sem.at[number],
            recv_sem=self.recv_sem.at[number],
            device_id=device,
            device_id_type=MESH,
        ).wait_recv()

    def finish(self):
        for copy in self.sent:
            copy.wait_send()


def planes(ref, piece, part=None):
    if part is None:
        return ref.at[pl.ds(piece * ROWS, ROWS)]
    return ref.at[pl.ds(piece * ROWS + part * HALF, HALF)]


def greet(me):
    barrier = pltpu.get_barrier_semaphore()
    near = [me.device(dx=1), me.device(dx=3), me.device(dy=1), me.device(dy=3),
            me.device(dz=1), me.device(dz=3), me.device(dx=2), me.device(flip=True)]
    for other in near:
        pl.semaphore_signal(barrier, inc=1, device_id=other, device_id_type=MESH)
    for k in range(1, 4):
        for other in (align_to(me, k), align_from(me, k)):
            pl.semaphore_signal(barrier, inc=1, device_id=other, device_id_type=MESH)

    @pl.when(jnp.logical_not(me.stays))
    def _():
        for other in (align_to(me, 0), align_from(me, 0)):
            pl.semaphore_signal(barrier, inc=1, device_id=other, device_id_type=MESH)
        pl.semaphore_wait(barrier, len(near) + 8)

    @pl.when(me.stays)
    def _():
        pl.semaphore_wait(barrier, len(near) + 6)


def align_to(me, step):
    band = ((me.band + me.z) % 2) * 2 + me.z // 2
    return (band, me.half * 16 + me.band * 4 + (me.y + step) % 4)


def align_z(me, x, core):
    return core * 2 + (x + me.z) % 2


def align_from(me, step):
    return (me.z, me.half * 16 + align_z(me, me.x, me.core) * 4 + (me.y - step) % 4)


class Tree:
    def __init__(self, me, mail, full, half, first):
        self.me, self.mail, self.full, self.half = me, mail, full, half
        self.first = first
        self.box = {}

    def off(self, f, s):
        return dict(dy=f % 4, dz=s % 4) if self.first == "y" else dict(dy=s % 4, dz=f % 4)

    def ref(self, f, s, part=None):
        return planes(self.full, self.me.piece(self.half, **self.off(f, s)), part)

    def push(self, key, src, f, s, df, ds, part=None):
        dst = self.ref(f, s, part)
        self.box[key] = self.mail.send(dst if src is None else src, dst, self.me.device(**self.off(df, ds)))

    def take(self, key, f, s, part=None):
        self.mail.arrive(self.box[key], self.ref(f, s, part), self.me.device(**self.off(0, 0)))

    def start(self, src):
        for d in (1, -1):
            self.push(("f", d), src, 0, 0, d, 0)
        for d in (1, -1):
            self.push(("s", 0, d), src, 0, 0, 0, d)

    def row(self):
        for d in (1, -1):
            self.take(("f", d), -d, 0)
            part = 0 if d == 1 else 1
            self.push(("f2", d), None, -d, 0, d, 0, part)
            for e in (1, -1):
                self.push(("s", -d, e), None, -d, 0, 0, e)

    def column(self, f):
        for e in (1, -1):
            self.take(("s", f, e), f, -e)
            part = 0 if e == 1 else 1
            self.push(("s2", f, e), None, f, -e, 0, e, part)

    def far(self):
        for d in (1, -1):
            self.take(("f2", d), 2, 0, 0 if d == 1 else 1)
        for e in (1, -1):
            self.push(("s", 2, e), None, 2, 0, 0, e)

    def last(self, f):
        for e in (1, -1):
            self.take(("s2", f, e), f, 2, 0 if e == 1 else 1)


def split(v):
    high = v.astype(jnp.bfloat16)
    return high, (v - high.astype(jnp.float32)).astype(jnp.bfloat16)


def times(v, table):
    r = jnp.dot(jnp.concatenate(split(v), axis=1), table, preferred_element_type=jnp.float32)
    return r[:, :GRID] + r[:, GRID:]


def under(table, va, vb):
    (ha, la), (hb, lb) = split(va), split(vb)
    values = jnp.concatenate([jnp.concatenate([ha, hb], axis=1), jnp.concatenate([la, lb], axis=1)], axis=0)
    r = jnp.dot(table, values, preferred_element_type=jnp.float32)
    r = r[:GRID] + r[GRID:]
    return r[:, :GRID], r[:, GRID:]


def gather(me, mail, res_ref, blk_ref, rfull, sfull, local_sem, fetches, forward):
    send_sem, recv_sem = mail.send_sem, mail.recv_sem
    h = me.half
    mine = me.piece(h)

    def spiece(dx, flip, t):
        x = (me.x + dx) % 4
        core = 1 - me.core if flip else me.core
        return (x // 2) * 16 + align_z(me, x, core) * 4 + (me.y + t) % 4

    swap = mail.send(res_ref.at[1 - h], planes(rfull, mine), me.device(dx=2))
    order = (0, 1, 3, 2)
    align_no = {}
    for t in order:
        number = mail.count
        mail.count += 1
        align_no[t] = number
        src = blk_ref.at[(me.y + t) % 4]
        dst = planes(sfull, mine)

        def remote(src=src, dst=dst, t=t, number=number):
            return pltpu.make_async_remote_copy(
                src_ref=src, dst_ref=dst, send_sem=send_sem.at[number], recv_sem=recv_sem.at[number],
                device_id=align_to(me, t), device_id_type=MESH)
        if t:
            copy = remote()
            copy.start()
            mail.sent.append(copy)
        else:
            @pl.when(jnp.logical_not(me.stays))
            def _():
                remote().start()

            @pl.when(me.stays)
            def _():
                pltpu.make_async_copy(src, dst, local_sem.at[1]).start()
            zero = (remote, src, dst)
    tree_a = Tree(me, mail, rfull, h, "y")
    tree_b = Tree(me, mail, rfull, 1 - h, "z")
    tree_a.start(res_ref.at[h])
    own = pltpu.make_async_copy(res_ref.at[h], planes(rfull, mine), local_sem.at[0])
    own.start()
    mail.arrive(swap, planes(rfull, me.piece(1 - h)), me.device(dx=2))
    tree_b.start(None)

    xs = {}
    backs = [-t % 4 for t in order]
    trees = (tree_a, tree_b)

    def collected():
        for t in order:
            back = -t % 4
            dst = planes(sfull, spiece(0, False, back))
            if t:
                mail.arrive(align_no[t], dst, align_from(me, t))
            else:
                @pl.when(jnp.logical_not(me.stays))
                def _():
                    zero[0]().wait_recv()

                @pl.when(me.stays)
                def _():
                    pltpu.make_async_copy(zero[1], zero[2], local_sem.at[1]).wait()
            for d in (1, -1):
                xs[("x", d, back)] = mail.send(dst, dst, me.device(dx=d))

    def beside():
        for t in backs:
            ref = planes(sfull, spiece(0, False, t))
            xs[("c", 0, t)] = mail.send(ref, ref, me.device(flip=True))
        for t in backs:
            for d in (1, -1):
                ref = planes(sfull, spiece(-d, False, t))
                mail.arrive(xs[("x", d, t)], ref, me.device(dx=-d))
                part = 0 if d == 1 else 1
                ref2 = planes(sfull, spiece(-d, False, t), part)
                xs[("x2", d, t)] = mail.send(ref2, ref2, me.device(dx=d))
                xs[("c", -d, t)] = mail.send(ref, ref, me.device(flip=True))

    def across():
        for t in backs:
            for d in (1, -1):
                ref2 = planes(sfull, spiece(2, False, t), 0 if d == 1 else 1)
                mail.arrive(xs[("x2", d, t)], ref2, me.device(dx=-d))
            ref = planes(sfull, spiece(2, False, t))
            xs[("c", 2, t)] = mail.send(ref, ref, me.device(flip=True))

    def column(*offsets):
        for f in offsets:
            for tree in trees:
                tree.column(f)

    def ready(late):
        for dx in (0, -1, 1, 2):
            x = (me.x + dx) % 4
            same = x // 2 == h
            close = align_z(me, x, me.core) != (me.z + 2) % 4
            whole = jnp.logical_and(same, jnp.logical_not(close) if late else close)

            @pl.when(whole)
            def _():
                forward([spiece(dx, False, t) for t in range(4)])

            @pl.when(jnp.logical_not(same))
            def _():
                forward([spiece(dx, False, t) for t in ((2,) if late else (0, 1, 3))])

    steps = {
        "own": lambda: [copy.wait() for copy in (own, *fetches)],
        "row": lambda: [tree.row() for tree in trees],
        "far": lambda: [tree.far() for tree in trees],
        "c0": lambda: column(0),
        "c1": lambda: column(-1, 1),
        "c2": lambda: column(2),
        "last": lambda: [tree.last(f) for f in (0, -1, 1, 2) for tree in trees],
        "early": lambda: ready(False),
        "s0": collected,
        "s1": beside,
        "s2": across,
    }
    for step in STEPS:
        steps[step]()
    ready(True)
    for dx in (0, -1, 1, 2):
        for t in backs:
            mail.arrive(xs[("c", dx, t)], planes(sfull, spiece(dx, True, t)), me.device(flip=True))
        forward([spiece(dx, True, t) for t in backs])

    def finish():
        @pl.when(jnp.logical_not(me.stays))
        def _():
            zero[0]().wait_send()

    return finish


class Sum:
    def __init__(self, me, mail, term, near_s, far_s, near_f, far_f, half, first):
        self.me, self.mail, self.term = me, mail, term
        self.near_s, self.far_s, self.near_f, self.far_f = near_s, far_s, near_f, far_f
        self.half, self.first = half, first
        self.box = {}

    def off(self, f, s):
        return dict(dy=f % 4, dz=s % 4) if self.first == "y" else dict(dy=s % 4, dz=f % 4)

    def ref(self, f, s, part=None):
        return planes(self.term, self.me.piece(self.half, **self.off(f, s)), part)

    def slots(self, d, f=None):
        n = 0 if d == 1 else 1
        if f is None:
            return self.far_f.at[n], self.near_f.at[n]
        return self.far_s.at[f % 4, n], self.near_s.at[f % 4, n]

    def post(self, key, src, dst, df, ds):
        self.box[key] = self.mail.send(src, dst, self.me.device(**self.off(df, ds)))

    def add(self, key, into, slot):
        self.mail.arrive(self.box[key], slot, self.me.device())
        into[...] += slot[...]

    def far_column(self, f):
        for e in (1, -1):
            self.post(("a", f, e), self.ref(f, 2, 0 if e == 1 else 1), self.slots(e, f)[0], 0, e)

    def near_column(self, f):
        for e in (1, -1):
            self.add(("a", f, e), self.ref(f, e, 0 if e == 1 else 1), self.slots(e, f)[0])
            self.post(("b", f, e), self.ref(f, e), self.slots(e, f)[1], 0, e)

    def own_column(self, f):
        for e in (1, -1):
            self.add(("b", f, e), self.ref(f, 0), self.slots(e, f)[1])

    def far_row(self):
        for d in (1, -1):
            self.post(("c", d), self.ref(2, 0, 0 if d == 1 else 1), self.slots(d)[0], d, 0)

    def near_row(self, d):
        self.add(("c", d), self.ref(d, 0, 0 if d == 1 else 1), self.slots(d)[0])
        self.post(("d", d), self.ref(d, 0), self.slots(d)[1], d, 0)

    def own_row(self):
        for d in (1, -1):
            self.add(("d", d), self.ref(0, 0), self.slots(d)[1])


def kernel(res_ref, blk_ref, occ_ref, tables_ref, out_ref, right_ref, right_t_ref, left_ref, left_t_ref,
           rfull, sfull, term, work, near_s, far_s, near_f, far_f, send_sem, recv_sem, local_sem):
    me = Place()
    fetches = [
        pltpu.make_async_copy(tables_ref.at[n], ref, local_sem.at[2 + n])
        for n, ref in enumerate((right_ref, right_t_ref, left_ref, left_t_ref))
    ]
    for fetch in fetches:
        fetch.start()
    greet(me)
    mail = Mail(send_sem, recv_sem)
    h = me.half
    weight = -occ_ref[me.z * 4 + me.y]

    def units(pieces, n):
        return [pl.multiple_of(piece * ROWS + n * 2 * GRID, 2 * GRID) for piece in pieces]

    def pitched(start):
        first = pl.multiple_of(start // GRID * PITCH, 8)
        return pl.ds(first, GRID), pl.ds(pl.multiple_of(first + PITCH, 8), GRID)

    def forward(pieces):
        @pl.loop(0, PLANES // 2)
        def _(n):
            for start in units(pieces, n):
                rows = pl.ds(start, 2 * GRID)
                v = times(rfull[rows, :] * sfull[rows, :], right_ref[...])
                va, vb = under(left_t_ref[...], v[:GRID], v[GRID:])
                one, two = pitched(start)
                work[one, :] = va
                work[two, :] = vb

    def backward(pieces):
        @pl.loop(0, PLANES // 2)
        def _(n):
            starts = units(pieces, n)
            held = [[work[rows, :] for rows in pitched(start)] for start in starts]
            results = []
            for start, values in zip(starts, held):
                va, vb = under(left_ref[...], *values)
                v = times(jnp.concatenate([va, vb], axis=0), right_t_ref[...])
                results.append(v * (sfull[pl.ds(start, 2 * GRID), :] * weight))
            for start, v in zip(starts, results):
                term[pl.ds(start, 2 * GRID), :] = v

    finish = gather(me, mail, res_ref, blk_ref, rfull, sfull, local_sem, fetches, forward)

    def wave_sq(index):
        signed = jnp.minimum(index, GRID - index).astype(jnp.float32) * (2.0 * math.pi / GRID)
        return signed * signed

    shape = (GRID, GRID)
    base = wave_sq(lax.broadcasted_iota(jnp.int32, shape, 0)) + wave_sq(lax.broadcasted_iota(jnp.int32, shape, 1)) + KAPPA_SQ

    @pl.loop(0, GRID // (2 * DEEP))
    def _(n):
        indices = [(n * 2 * DEEP + 2 * k, n * 2 * DEEP + 2 * k + 1) for k in range(DEEP)]
        held = [[work[pl.ds(i, GRID, stride=PITCH), :] for i in pair] for pair in indices]
        results = []
        for pair, values in zip(indices, held):
            values = under(left_t_ref[...], *values)
            values = [v * (4.0 * math.pi / (base + wave_sq(i))) for i, v in zip(pair, values)]
            results.append(under(left_ref[...], *values))
        for pair, values in zip(indices, results):
            for i, v in zip(pair, values):
                work[pl.ds(i, GRID, stride=PITCH), :] = v

    sums = [
        Sum(me, mail, term, near_s.at[n], far_s.at[n], near_f.at[n], far_f.at[n], half, first)
        for n, (half, first) in enumerate(((1 - h, "z"), (h, "y")))
    ]
    def pieces(s, f, off):
        return [me.piece(s.half, **s.off(f, off))]

    def far(f):
        backward([p for s in sums for p in pieces(s, f, 2)])
        for s in sums:
            s.far_column(f)

    def near(f):
        backward([p for s in sums for e in (1, -1) for p in pieces(s, f, e)])
        for s in sums:
            s.near_column(f)

    def own(f):
        backward([p for s in sums for p in pieces(s, f, 0)])
        for s in sums:
            s.own_column(f)
        for s in sums:
            if f == 2:
                s.far_row()
            elif f:
                s.near_row(f)

    for step, f in (
        (far, 2), (far, 1), (far, -1), (near, 2), (far, 0), (near, 1), (near, -1), (own, 2),
        (near, 0), (own, 1), (own, -1), (own, 0),
    ):
        step(f)
    sums[0].own_row()
    swap = mail.send(planes(term, me.piece(1 - h)), out_ref.at[h], me.device(dx=2))
    sums[1].own_row()
    mail.arrive(swap, out_ref.at[1 - h], me.device(dx=2))
    mail.finish()
    out_ref[h] = planes(term, me.piece(h))[...]
    finish()


MESSAGES = 77 + 41


def basis():
    points = np.arange(GRID)
    freqs = np.minimum(points, GRID - points)
    angles = 2.0 * np.pi * ((points[:, None] * freqs[None, :]) % GRID) / GRID
    table = np.where(points[None, :] > GRID // 2, np.sin(angles), np.cos(angles)) * np.sqrt(2.0 / GRID)
    table[:, 0] /= np.sqrt(2.0)
    table[:, GRID // 2] /= np.sqrt(2.0)
    return table


def tables():
    b = basis()

    def parts(t):
        high = t.astype(ml_dtypes.bfloat16)
        return high, (t - high.astype(np.float64)).astype(ml_dtypes.bfloat16)

    def right(t):
        high, low = parts(t)
        return np.block([[high, low], [high, np.zeros_like(low)]])

    def left(t):
        high, low = parts(t)
        return np.block([[high, high], [low, np.zeros_like(low)]])

    return jnp.asarray(np.stack([right(b), right(b.T), left(b), left(b.T)]))


def per_device(resident, blocks, occupation):
    vmem = pl.BlockSpec(memory_space=pltpu.VMEM)
    hbm = pl.BlockSpec(memory_space=pl.ANY)
    full = pltpu.VMEM((GRID * GRID, GRID), jnp.float32)
    out = pl.pallas_call(
        kernel,
        out_shape=jax.ShapeDtypeStruct((2, ROWS, GRID), jnp.float32),
        in_specs=[hbm, hbm, pl.BlockSpec(memory_space=pltpu.SMEM), hbm],
        out_specs=vmem,
        scratch_shapes=[
            *[pltpu.VMEM((2 * GRID, 2 * GRID), jnp.bfloat16)] * 4,
            full,
            full,
            full,
            pltpu.VMEM((GRID * PITCH, GRID), jnp.float32),
            pltpu.VMEM((2, 4, 2, ROWS, GRID), jnp.float32),
            pltpu.VMEM((2, 4, 2, HALF, GRID), jnp.float32),
            pltpu.VMEM((2, 2, ROWS, GRID), jnp.float32),
            pltpu.VMEM((2, 2, HALF, GRID), jnp.float32),
            pltpu.SemaphoreType.DMA((MESSAGES,)),
            pltpu.SemaphoreType.DMA((MESSAGES,)),
            pltpu.SemaphoreType.DMA((6,)),
        ],
        compiler_params=pltpu.CompilerParams(
            collective_id=0, has_side_effects=True, vmem_limit_bytes=56 * 2**20
        ),
        cost_estimate=pl.CostEstimate(flops=13 * 10**9, bytes_accessed=10**7, transcendentals=0),
        name="exchange",
    )(
        resident.reshape(2, ROWS, GRID),
        blocks.reshape(4, ROWS, GRID),
        occupation,
        tables(),
    )
    return out.reshape(2, PLANES, GRID, GRID)


def solution(mesh):
    placed = (P("band", "slab", None, None), P("band", "slab", None, None), P())
    return jax.shard_map(
        per_device,
        mesh=mesh,
        in_specs=placed,
        out_specs=P("band", "slab", None, None),
        check_vma=False,
    )
```
